512 devices in a mesh: prow: 16 (over z), pcol: 32 (over y, x, core).
Axes of the slice: x: 4, y: 4, z: 16, core: 2. Of those that a mesh axis runs over, the one named last changes fastest.
Arguments:
- matrix: float32 [2, 16, 256, 32, 256], P(None, 'prow', None, 'pcol'), may hold values from -6 to 6, as said below
Outputs:
- factored: float32 [2, 16, 256, 32, 256], P(None, 'prow', None, 'pcol')
The draws below stay inside these ranges and needn't reach their ends.
Inputs may be any that keep to these rules, and one draw needn't show every extreme that they name: `matrix`: in the first 3 diagonal blocks every diagonal entry lies between 1.3 and 3.2, and diag(1/d) times the off-diagonal part of each such block has spectral norm below about 0.7.
All inputs are finite; a program needn't handle non-finite values.
Results may differ from the reference program's by a relative error of at most 0.0001.
Values sent between devices are 32-bit elements; how exact they have to be, the bound alone decides.
A program may use at most 64 MiB of HBM per device.

```python
import math
import jax
import jax.numpy as jnp
from jax import lax

B = 256
RB_DEV = 2
PANELS = 3
PROWS = 16
PCOLS = 32


def draw_matrix(key, part):
    first_key, second_key = jax.random.split(key)
    shape = (RB_DEV, PROWS, B, PCOLS, B)
    base = jnp.clip(jax.random.normal(first_key, shape, jnp.float32), -6.0, 6.0)
    block_row = (jnp.arange(RB_DEV)[:, None] * PROWS + jnp.arange(PROWS)[None, :]).reshape(RB_DEV, PROWS, 1, 1, 1)
    block_col = jnp.arange(PCOLS).reshape(1, 1, 1, PCOLS, 1)
    head = (block_row < PANELS) & (block_col < PANELS)
    upper = (block_row < PANELS) & (block_col >= PANELS)
    scale = jnp.where(head, 0.5 / math.sqrt(B), jnp.where(upper, 0.1, 1.0))
    inner_row = jnp.arange(B).reshape(1, 1, B, 1, 1)
    inner_col = jnp.arange(B).reshape(1, 1, 1, 1, B)
    on_diag = head & (block_row == block_col) & (inner_row == inner_col)
    lift = jax.random.uniform(second_key, shape, jnp.float32, 1.5, 3.0)
    return base * scale + jnp.where(on_diag, lift, 0.0)


def setup_inputs(seed: int = 0) -> dict:
    keys = jax.random.split(jax.random.key(seed), 2)
    matrix = draw_matrix(jax.random.fold_in(keys[1], 71), 0)
    return {"matrix": matrix}


def invert(block):
    scales = 1.0 / jnp.diagonal(block)
    first = 2.0 * jnp.diag(scales) - scales[:, None] * block * scales[None, :]
    inner = jnp.dot(block, first, precision=lax.Precision.HIGHEST)
    return 2.0 * first - jnp.dot(first, inner, precision=lax.Precision.HIGHEST)


def reference(matrix):
    shape = matrix.shape
    full = matrix.reshape(shape[0] * shape[1] * shape[2], shape[3] * shape[4])
    for panel in range(PANELS):
        lower = panel * B
        upper = lower + B
        inverse = invert(full[lower:upper, lower:upper])
        factors = jnp.dot(full[upper:, lower:upper], inverse, precision=lax.Precision.HIGHEST)
        update = jnp.dot(factors, full[lower:upper, upper:], precision=lax.Precision.HIGHEST)
        full = full.at[upper:, upper:].set(full[upper:, upper:] - update)
        full = full.at[upper:, lower:upper].set(factors)
        full = full.at[lower:upper, lower:upper].set(inverse)
    return full.reshape(shape)
```

```python
import functools

import jax
import jax.numpy as jnp
from jax import lax
from jax.experimental import pallas as pl
from jax.experimental.pallas import tpu as pltpu
from jax.sharding import PartitionSpec as P

B = 256
PANELS = 3
NP = 16
NQ = 32
NC = NQ // 2
S = B // NQ
CHUNKS = 8
CR = B // CHUNKS
MESH = pl.DeviceIdType.MESH


def split(value):
    high = value.astype(jnp.bfloat16)
    return high, (value - high.astype(jnp.float32)).astype(jnp.bfloat16)


def dot3(left, right):
    dot = functools.partial(jnp.dot, preferred_element_type=jnp.float32)
    return dot(left[0], right[0]) + (dot(left[0], right[1]) + dot(left[1], right[0]))


def invert(block):
    row = lax.broadcasted_iota(jnp.int32, (B, B), 0)
    col = lax.broadcasted_iota(jnp.int32, (B, B), 1)
    eye = row == col
    diagonal = jnp.where(eye, block, 0.0)
    down = 1.0 / jnp.sum(diagonal, axis=1, keepdims=True)
    across = 1.0 / jnp.sum(diagonal, axis=0, keepdims=True)
    first = jnp.where(eye, 2.0 * down, 0.0) - down * block * across
    parts = split(first)
    inner = dot3(split(block), parts)
    return 2.0 * first - dot3(parts, split(inner))


def kernel(
    x_ref,
    out_ref,
    rs,
    rows,
    hs,
    head,
    cols,
    fact,
    upper,
    sc_send,
    sc_recv,
    ra_send,
    ra_recv,
    hz_send,
    hz_recv,
    ha_send,
    ha_recv,
    zu_send,
    zd_send,
    z_recv,
    cc_send,
    cc_recv,
):
    p = lax.axis_index("prow")
    q = lax.axis_index("pcol")
    core = lax.rem(q, 2)
    chip = q // 2
    partner = q + 1 - 2 * core

    def remote(src, dst, send, recv, row, col):
        return pltpu.make_async_remote_copy(
            src_ref=src, dst_ref=dst, send_sem=send, recv_sem=recv, device_id=(row, col), device_id_type=MESH
        )

    def mine(t):
        return pl.ds(pl.multiple_of((lax.rem(t, 2) * NC + t // 2) * S, S), S)

    barrier = pltpu.get_barrier_semaphore()

    @pl.loop(1, NQ)
    def _(j):
        pl.semaphore_signal(barrier, inc=1, device_id=(p, lax.rem(q + j, NQ)), device_id_type=MESH)

    @pl.loop(1, NP)
    def _(j):
        pl.semaphore_signal(barrier, inc=1, device_id=(lax.rem(p + j, NP), q), device_id_type=MESH)

    pl.semaphore_wait(barrier, NQ - 1 + NP - 1)

    def scatter(j):
        t = lax.rem(q + j, NQ)
        return remote(x_ref.at[:, mine(t)], rs.at[q], sc_send.at[j], sc_recv.at[q], p, t)

    @pl.when(q < PANELS)
    def _():
        rs[q] = x_ref[:, mine(q)]

        @pl.loop(1, NQ)
        def _(j):
            scatter(j).start()

    for k in range(PANELS):

        @pl.when(q != k)
        def _():
            remote(x_ref.at[:, pl.ds(0, S)], rs.at[k], sc_send.at[0], sc_recv.at[k], p, partner).wait_recv()

    def head_along(j):
        return remote(rs.at[:, 0], hs.at[p], hz_send.at[j], hz_recv.at[p], lax.rem(p + j, NP), q)

    @pl.when(p < PANELS)
    def _():
        hs[p] = rs[:, 0]

        @pl.loop(1, NP)
        def _(j):
            head_along(j).start()

    def gather(src, dst, send, recv, j):
        return remote(src, dst.at[core, chip], send.at[j], recv.at[chip], p, lax.rem(q + 2 * j, NQ))

    rows[core, chip] = rs[...]

    @pl.loop(1, NC)
    def _(j):
        gather(rs, rows, ra_send, ra_recv, j).start()

    for k in range(PANELS):

        @pl.when(p != k)
        def _():
            remote(rs.at[:, 0], hs.at[k], hz_send.at[0], hz_recv.at[k], lax.rem(p + 1, NP), q).wait_recv()

    head[core, chip] = hs[...]

    @pl.loop(1, NC)
    def _(j):
        gather(hs, head, ha_send, ha_recv, j).start()

    @pl.when(p < PANELS)
    def _():
        cols[p] = x_ref[0]

    def chunk(i):
        k = lax.rem(i, PANELS)
        c = i // PANELS
        odd = lax.rem(c, 2)
        reach = (1 - odd) * (11 - c // 2) + odd * (4 + c // 2)
        away = lax.rem(p - k + NP, NP)
        piece = cols.at[k, pl.ds(pl.multiple_of(c * CR, CR), CR)]
        up = remote(piece, piece, zu_send.at[i], z_recv.at[i], lax.rem(p + 1, NP), q)
        down = remote(piece, piece, zd_send.at[i], z_recv.at[i], lax.rem(p + NP - 1, NP), q)
        goes_up = away < reach
        goes_down = (away == 0) | (away > reach + 1)
        return away, up, down, goes_up, goes_down

    @pl.loop(0, PANELS * CHUNKS)
    def _(i):
        away, up, down, goes_up, goes_down = chunk(i)

        @pl.when(away != 0)
        def _():
            up.wait_recv()

        @pl.when(goes_up)
        def _():
            up.start()

        @pl.when(goes_down)
        def _():
            down.start()

    def across(buffer, i):
        return remote(buffer.at[core], buffer.at[core], cc_send.at[i], cc_recv.at[i], p, partner)

    @pl.loop(1, NC)
    def _(j):
        remote(rs, rows.at[core, 0], ra_send.at[0], ra_recv.at[lax.rem(chip + j, NC)], p, partner).wait_recv()

    across(rows, 0).start()

    @pl.loop(1, NC)
    def _(j):
        remote(hs, head.at[core, 0], ha_send.at[0], ha_recv.at[lax.rem(chip + j, NC)], p, partner).wait_recv()

    across(head, 1).start()
    across(head, 1).wait_recv()

    def block(i, j):
        return head[:, :, i, j].reshape(B, B)

    a = {(i, j): block(i, j) for i in range(PANELS) for j in range(PANELS)}
    halves = {}
    for k in range(PANELS):
        inverse = invert(a[k, k])
        fact[k, k] = inverse
        halves[k, k] = split(inverse)
        for j in range(k + 1, PANELS):
            fact[k, j] = a[k, j]
            halves[k, j] = split(a[k, j])
        for i in range(k + 1, PANELS):
            factor = dot3(split(a[i, k]), halves[k, k])
            fact[i, k] = factor
            halves[i, k] = split(factor)
            for j in range(k + 1, PANELS):
                a[i, j] = a[i, j] - dot3(halves[i, k], halves[k, j])

    is_panel = q < PANELS
    eye = (
        lax.broadcasted_iota(jnp.int32, (B, B), 0) == lax.broadcasted_iota(jnp.int32, (B, B), 1)
    ).astype(jnp.float32)
    y = []
    for i in range(PANELS):
        value = cols[i]
        for k in range(i):
            value = value - dot3(halves[i, k], y[k])
        upper[i] = value
        y.append(split(value))

    right = [None] * PANELS
    for i in reversed(range(PANELS)):
        value = jnp.where(is_panel, jnp.where(q == i, eye, 0.0), upper[i])
        for k in range(i + 1, PANELS):
            value = value - dot3(halves[i, k], right[k])
        right[i] = split(dot3(halves[i, i], split(value)))

    across(rows, 0).wait_recv()
    keep = jnp.where(is_panel, 0.0, 1.0)
    sign = jnp.where(is_panel, 1.0, -1.0)
    for b in range(2):
        total = jnp.zeros((B, B), jnp.float32)
        for k in range(PANELS):
            total = total + dot3(split(rows[:, :, k, b].reshape(B, B)), right[k])
        out_ref[b] = keep * x_ref[b] + sign * total

    @pl.when((p < PANELS) & is_panel)
    def _():
        out_ref[0] = fact[lax.rem(p, PANELS), lax.rem(q, PANELS)]

    @pl.when((p < PANELS) & (q >= PANELS))
    def _():
        out_ref[0] = upper[lax.rem(p, PANELS)]

    @pl.when(q < PANELS)
    def _():
        @pl.loop(1, NQ)
        def _(j):
            scatter(j).wait_send()

    @pl.when(p < PANELS)
    def _():
        @pl.loop(1, NP)
        def _(j):
            head_along(j).wait_send()

    @pl.loop(1, NC)
    def _(j):
        gather(rs, rows, ra_send, ra_recv, j).wait_send()
        gather(hs, head, ha_send, ha_recv, j).wait_send()

    @pl.loop(0, PANELS * CHUNKS)
    def _(i):
        _, up, down, goes_up, goes_down = chunk(i)

        @pl.when(goes_up)
        def _():
            up.wait_send()

        @pl.when(goes_down)
        def _():
            down.wait_send()

    across(rows, 0).wait_send()
    across(head, 1).wait_send()


def body(matrix):
    shape = matrix.shape
    f32 = jnp.float32
    dma = pltpu.SemaphoreType.DMA
    out = pl.pallas_call(
        kernel,
        out_shape=jax.ShapeDtypeStruct((2, B, B), f32),
        in_specs=[pl.BlockSpec(memory_space=pltpu.VMEM)],
        out_specs=pl.BlockSpec(memory_space=pltpu.VMEM),
        scratch_shapes=[
            pltpu.VMEM((PANELS, 2, S, B), f32),
            pltpu.VMEM((2, NC, PANELS, 2, S, B), f32),
            pltpu.VMEM((PANELS, PANELS, S, B), f32),
            pltpu.VMEM((2, NC, PANELS, PANELS, S, B), f32),
            pltpu.VMEM((PANELS, B, B), f32),
            pltpu.VMEM((PANELS, PANELS, B, B), f32),
            pltpu.VMEM((PANELS, B, B), f32),
            dma((NQ,)),
            dma((PANELS,)),
            dma((NC,)),
            dma((NC,)),
            dma((NP,)),
            dma((PANELS,)),
            dma((NC,)),
            dma((NC,)),
            dma((PANELS * CHUNKS,)),
            dma((PANELS * CHUNKS,)),
            dma((PANELS * CHUNKS,)),
            dma((2,)),
            dma((2,)),
        ],
        compiler_params=pltpu.CompilerParams(
            collective_id=0, has_side_effects=True, vmem_limit_bytes=48 * 1024 * 1024
        ),
    )(matrix.reshape(2, B, B))
    return out.reshape(shape)


def solution(mesh):
    spec = P(None, "prow", None, "pcol", None)
    return jax.shard_map(body, mesh=mesh, in_specs=(spec,), out_specs=spec, check_vma=False)
```

```python
import functools

import jax
import jax.numpy as jnp
from jax import lax
from jax.experimental import pallas as pl
from jax.experimental.pallas import tpu as pltpu
from jax.sharding import PartitionSpec as P

B = 256
PANELS = 3
NP = 16
NQ = 32
NC = NQ // 2
S = B // NC
CHUNKS = 8
CR = B // CHUNKS
MESH = pl.DeviceIdType.MESH
STEPS0 = (2, 1, -1, -2)
STEPS1 = (4, 1, -1, -2, -4)


def split(value):
    high = value.astype(jnp.bfloat16)
    return high, (value - high.astype(jnp.float32)).astype(jnp.bfloat16)


def dot3(left, right):
    dot = functools.partial(jnp.dot, preferred_element_type=jnp.float32)
    return dot(left[0], right[0]) + (dot(left[0], right[1]) + dot(left[1], right[0]))


def invert(block):
    row = lax.broadcasted_iota(jnp.int32, (B, B), 0)
    col = lax.broadcasted_iota(jnp.int32, (B, B), 1)
    eye = row == col
    diagonal = jnp.where(eye, block, 0.0)
    down = 1.0 / jnp.sum(diagonal, axis=1, keepdims=True)
    across = 1.0 / jnp.sum(diagonal, axis=0, keepdims=True)
    first = jnp.where(eye, 2.0 * down, 0.0) - down * block * across
    parts = split(first)
    inner = dot3(split(block), parts)
    return 2.0 * first - dot3(parts, split(inner))


def wrap(p):
    return lax.rem(p + 2 * NP, NP)


def col_edge(step, away):
    if step == 2:
        return (away == 0) | (away == 2) | (away == 4) | (away == 6)
    if step == -2:
        return (away == 0) | (away == 14) | (away == 12)
    if step == -1:
        return (away == 2) | (away == 4) | (away == 6) | (away == 8)
    return (away == 8) | (away == 14) | (away == 12) | (away == 10)


def edge0(step, p):
    found = col_edge(step, wrap(p))
    for k in range(1, PANELS):
        found = found | col_edge(step, wrap(p - k))
    return found


def edge1(step, p):
    near = lax.rem(p, 4)
    if step == 4:
        return (near < PANELS) & (p < 8)
    if step == -4:
        return p < PANELS
    return near < PANELS


def kernel(
    x_ref,
    out_ref,
    rs,
    rows,
    hs,
    head,
    cols,
    fact,
    upper,
    ready0,
    ready1,
    sc_send,
    sc_recv,
    ra_send,
    ra_recv,
    hz_send,
    hz_recv,
    ha_send,
    ha_recv,
    z_send,
    z_recv,
    own_send,
    own_recv,
    zc_send,
    zc_recv,
    cc_send,
    cc_recv,
):
    p = lax.axis_index("prow")
    q = lax.axis_index("pcol")
    core = lax.rem(q, 2)
    chip = q // 2
    partner = q + 1 - 2 * core
    is_zero = core == 0
    is_one = core == 1
    is_root = p < PANELS
    scatters = (q == 0) | (q == 2)

    def remote(src, dst, send, recv, row, col):
        return pltpu.make_async_remote_copy(
            src_ref=src, dst_ref=dst, send_sem=send, recv_sem=recv, device_id=(row, col), device_id_type=MESH
        )

    def signal(sem, row, col):
        pl.semaphore_signal(sem, inc=1, device_id=(row, col), device_id_type=MESH)

    def count(flag):
        return flag.astype(jnp.int32)

    barrier = pltpu.get_barrier_semaphore()

    def greet(steps, edge):
        for s in steps:
            child, parent = wrap(p + s), wrap(p - s)

            @pl.when(edge(s, p) & (p < child))
            def _():
                signal(barrier, child, q)

            @pl.when(edge(s, parent) & (parent > p))
            def _():
                signal(barrier, parent, q)

    def greetings(steps, edge):
        total = 0
        for s in steps:
            child, parent = wrap(p + s), wrap(p - s)
            total = total + count(edge(s, parent) & (parent < p)) + count(edge(s, p) & (child < p))
        return total

    def answer(steps, edge, ready):
        for i, s in enumerate(steps):
            parent = wrap(p - s)

            @pl.when(edge(s, parent) & (parent < p))
            def _():
                signal(ready.at[i], parent, q)

    def await_ready(steps, edge, ready, s):
        @pl.when(edge(s, p) & (p < wrap(p + s)))
        def _():
            pl.semaphore_wait(ready.at[steps.index(s)], 1)

    @pl.when(is_zero)
    def _():
        greet(STEPS0, edge0)

        @pl.when(scatters)
        def _():
            @pl.loop(0, NC)
            def _(j):
                signal(barrier, p, 2 * j + 1)

        @pl.when(jnp.logical_not(scatters))
        def _():
            signal(barrier, p, partner)

        pl.semaphore_wait(barrier, greetings(STEPS0, edge0) + 1 + (NC - 1) * count(scatters))
        answer(STEPS0, edge0, ready0)

    @pl.when(is_one)
    def _():
        greet(STEPS1, edge1)

        @pl.loop(1, NC)
        def _(j):
            signal(barrier, p, lax.rem(q + 2 * j, NQ))

        for t in (0, 2):

            @pl.when(partner != t)
            def _():
                signal(barrier, p, t)

        signal(barrier, p, partner)
        others = NC - 1 + 3 - count((partner == 0) | (partner == 2))
        pl.semaphore_wait(barrier, greetings(STEPS1, edge1) + others)
        answer(STEPS1, edge1, ready1)

    def scatter(t):
        piece = x_ref.at[:, pl.ds(pl.multiple_of(t * S, S), S)]
        return remote(piece, rs.at[lax.rem(q, PANELS)], sc_send.at[t], sc_recv.at[lax.rem(q, PANELS)], p, 2 * t + 1)

    def each_scatter(act):
        @pl.when(q < PANELS)
        def _():
            @pl.loop(0, NC)
            def _(t):
                @pl.when(2 * t + 1 != q)
                def _():
                    act(scatter(t))

    def own():
        return remote(x_ref.at[0], cols.at[1, lax.rem(p, PANELS)], own_send, own_recv, p, partner)

    @pl.when(is_one & is_root)
    def _():
        own().start()

    each_scatter(lambda copy: copy.start())

    def col_piece(i):
        return pl.ds(pl.multiple_of(i * CR, CR), CR)

    def col_copy(k, i, step):
        piece = cols.at[:, k, col_piece(i)]
        n = STEPS0.index(step)
        return remote(piece, piece, z_send.at[n, k * CHUNKS + i], z_recv.at[k * CHUNKS + i], wrap(p + step), q)

    def to_one(k, i):
        piece = cols.at[1, k, col_piece(i)]
        return remote(piece, piece, zc_send.at[k], zc_recv.at[k], p, partner)

    @pl.when(is_zero)
    def _():
        mine = lax.rem(p, PANELS)

        @pl.when(is_root)
        def _():
            cols[0, mine] = x_ref[0]
            own().wait_recv()

        for s in (2, 1, -1, -2):
            await_ready(STEPS0, edge0, ready0, s)
            if s in (2, -2):

                @pl.when(is_root)
                def _():
                    @pl.loop(0, CHUNKS)
                    def _(i):
                        col_copy(mine, i, s).start()

        @pl.loop(0, CHUNKS)
        def _(i):
            for k in reversed(range(PANELS)):
                away = wrap(p - k)

                @pl.when((lax.rem(away, 2) == 0) & (away != 0))
                def _():
                    col_copy(k, i, 2).wait_recv()
                    for s in STEPS0:

                        @pl.when(col_edge(s, away))
                        def _():
                            col_copy(k, i, s).start()

                    to_one(k, i).start()

        @pl.loop(0, CHUNKS)
        def _(i):
            for k in range(PANELS):

                @pl.when(lax.rem(wrap(p - k), 2) == 1)
                def _():
                    col_copy(k, i, 2).wait_recv()
                    to_one(k, i).start()

    def gather(src, dst, send, recv, j):
        return remote(src, dst.at[chip], send.at[j], recv.at[chip], p, lax.rem(q + 2 * j, NQ))

    def across(buffer, i, j):
        return remote(buffer.at[j], buffer.at[j], cc_send.at[i], cc_recv.at[i], p, partner)

    def whole(buffer, i):
        return remote(buffer, buffer, cc_send.at[i], cc_recv.at[i], p, partner)

    near = lax.rem(p, 4)
    mine4 = lax.rem(near, PANELS)
    anchor = near < PANELS

    def along(step):
        n = STEPS1.index(step)
        return remote(hs.at[mine4], hs.at[mine4], hz_send.at[n], hz_recv.at[mine4], wrap(p + step), q)

    def hand_over(src, buffer, recv, i):
        across(buffer, i, chip).start()

        @pl.loop(1, NC)
        def _(j):
            c = lax.rem(chip + j, NC)
            remote(src, buffer.at[c], ra_send.at[0], recv.at[c], p, partner).wait_recv()
            across(buffer, i, c).start()

    @pl.when(is_one)
    def _():
        @pl.when(q == 1)
        def _():
            rs[1] = x_ref[:, 0:S]

        for k in range(PANELS):

            @pl.when(q != k)
            def _():
                remote(x_ref.at[:, pl.ds(0, S)], rs.at[k], sc_send.at[0], sc_recv.at[k], p, partner).wait_recv()

        @pl.when(is_root)
        def _():
            hs[mine4] = rs[:, 0]

        @pl.when(anchor & jnp.logical_not(is_root))
        def _():
            along(4).wait_recv()

        for s in STEPS1:
            await_ready(STEPS1, edge1, ready1, s)

            @pl.when(edge1(s, p))
            def _():
                along(s).start()

        rows[chip] = rs[...]

        @pl.loop(1, NC)
        def _(j):
            gather(rs, rows, ra_send, ra_recv, j).start()

        for k in range(PANELS):

            @pl.when(near != k)
            def _():
                remote(hs.at[k], hs.at[k], hz_send.at[0], hz_recv.at[k], p, partner).wait_recv()

        head[chip] = hs[...]

        @pl.loop(1, NC)
        def _(j):
            gather(hs, head, ha_send, ha_recv, j).start()

        @pl.when(is_root)
        def _():
            cols[1, lax.rem(p, PANELS)] = x_ref[0]

        hand_over(rs, rows, ra_recv, 0)
        hand_over(hs, head, ha_recv, 1)

    @pl.when(is_zero)
    def _():
        whole(head, 1).wait_recv()

    def block(i, j):
        return head[:, i, j].reshape(B, B)

    a = {(i, j): block(i, j) for i in range(PANELS) for j in range(PANELS)}
    halves = {}
    for k in range(PANELS):
        inverse = invert(a[k, k])
        fact[k, k] = inverse
        halves[k, k] = split(inverse)
        for j in range(k + 1, PANELS):
            fact[k, j] = a[k, j]
            halves[k, j] = split(a[k, j])
        for i in range(k + 1, PANELS):
            factor = dot3(split(a[i, k]), halves[k, k])
            fact[i, k] = factor
            halves[i, k] = split(factor)
            for j in range(k + 1, PANELS):
                a[i, j] = a[i, j] - dot3(halves[i, k], halves[k, j])

    @pl.when(is_one)
    def _():
        for k in range(PANELS):

            @pl.when(p != k)
            def _():
                remote(cols.at[1, k], cols.at[1, k], zc_send.at[k], zc_recv.at[k], p, partner).wait_recv()

    is_panel = q < PANELS
    eye = (
        lax.broadcasted_iota(jnp.int32, (B, B), 0) == lax.broadcasted_iota(jnp.int32, (B, B), 1)
    ).astype(jnp.float32)
    y = []
    for i in range(PANELS):
        value = cols[core, i]
        for k in range(i):
            value = value - dot3(halves[i, k], y[k])
        upper[i] = value
        y.append(split(value))

    right = [None] * PANELS
    for i in reversed(range(PANELS)):
        value = jnp.where(is_panel, jnp.where(q == i, eye, 0.0), upper[i])
        for k in range(i + 1, PANELS):
            value = value - dot3(halves[i, k], right[k])
        right[i] = split(dot3(halves[i, i], split(value)))

    @pl.when(is_zero)
    def _():
        whole(rows, 0).wait_recv()

    keep = jnp.where(is_panel, 0.0, 1.0)
    sign = jnp.where(is_panel, 1.0, -1.0)
    for b in range(2):
        total = jnp.zeros((B, B), jnp.float32)
        for k in range(PANELS):
            total = total + dot3(split(rows[:, k, b].reshape(B, B)), right[k])
        out_ref[b] = keep * x_ref[b] + sign * total

    @pl.when(is_root & is_panel)
    def _():
        out_ref[0] = fact[lax.rem(p, PANELS), lax.rem(q, PANELS)]

    @pl.when(is_root & (q >= PANELS))
    def _():
        out_ref[0] = upper[lax.rem(p, PANELS)]

    each_scatter(lambda copy: copy.wait_send())

    @pl.when(is_zero)
    def _():
        for k in range(PANELS):
            away = wrap(p - k)
            for s in STEPS0:

                @pl.when(col_edge(s, away))
                def _():
                    @pl.loop(0, CHUNKS)
                    def _(i):
                        col_copy(k, i, s).wait_send()

            @pl.when(away != 0)
            def _():
                remote(cols.at[1, k], cols.at[1, k], zc_send.at[k], zc_recv.at[k], p, partner).wait_send()

    @pl.when(is_one)
    def _():
        @pl.when(is_root)
        def _():
            own().wait_send()

        for s in STEPS1:

            @pl.when(edge1(s, p))
            def _():
                along(s).wait_send()

        @pl.loop(1, NC)
        def _(j):
            gather(rs, rows, ra_send, ra_recv, j).wait_send()
            gather(hs, head, ha_send, ha_recv, j).wait_send()

        whole(rows, 0).wait_send()
        whole(head, 1).wait_send()


def body(matrix):
    shape = matrix.shape
    f32 = jnp.float32
    dma = pltpu.SemaphoreType.DMA
    out = pl.pallas_call(
        kernel,
        out_shape=jax.ShapeDtypeStruct((2, B, B), f32),
        in_specs=[pl.BlockSpec(memory_space=pltpu.VMEM)],
        out_specs=pl.BlockSpec(memory_space=pltpu.VMEM),
        scratch_shapes=[
            pltpu.VMEM((PANELS, 2, S, B), f32),
            pltpu.VMEM((NC, PANELS, 2, S, B), f32),
            pltpu.VMEM((PANELS, PANELS, S, B), f32),
            pltpu.VMEM((NC, PANELS, PANELS, S, B), f32),
            pltpu.VMEM((2, PANELS, B, B), f32),
            pltpu.VMEM((PANELS, PANELS, B, B), f32),
            pltpu.VMEM((PANELS, B, B), f32),
            pltpu.SemaphoreType.REGULAR((len(STEPS0),)),
            pltpu.SemaphoreType.REGULAR((len(STEPS1),)),
            dma((NC,)),
            dma((PANELS,)),
            dma((NC,)),
            dma((NC,)),
            dma((len(STEPS1),)),
            dma((PANELS,)),
            dma((NC,)),
            dma((NC,)),
            dma((len(STEPS0), PANELS * CHUNKS)),
            dma((PANELS * CHUNKS,)),
            dma,
            dma,
            dma((PANELS,)),
            dma((PANELS,)),
            dma((2,)),
            dma((2,)),
        ],
        compiler_params=pltpu.CompilerParams(
            collective_id=0, has_side_effects=True, vmem_limit_bytes=48 * 1024 * 1024
        ),
    )(matrix.reshape(2, B, B))
    return out.reshape(shape)


def solution(mesh):
    spec = P(None, "prow", None, "pcol", None)
    return jax.shard_map(body, mesh=mesh, in_specs=(spec,), out_specs=spec, check_vma=False)
```

```python
import functools

import jax
import jax.numpy as jnp
from jax import lax
from jax.experimental import pallas as pl
from jax.experimental.pallas import tpu as pltpu
from jax.sharding import PartitionSpec as P

B = 256
PANELS = 3
NP = 16
NQ = 32
NC = NQ // 2
S = B // NC // 2
SIDE = 4
CHUNKS = 8
CR = 2 * B // CHUNKS
WINDOW = 3
LAG = 3
MESH = pl.DeviceIdType.MESH
STEPS0 = (2, 1, -1, -2)
STEPS1 = (4, 1, -1, -2, -4)


def split(value):
    high = value.astype(jnp.bfloat16)
    return high, (value - high.astype(jnp.float32)).astype(jnp.bfloat16)


def dot3(left, right):
    dot = functools.partial(jnp.dot, preferred_element_type=jnp.float32)
    return dot(left[0], right[0]) + (dot(left[0], right[1]) + dot(left[1], right[0]))


def invert(block):
    row = lax.broadcasted_iota(jnp.int32, (B, B), 0)
    col = lax.broadcasted_iota(jnp.int32, (B, B), 1)
    eye = row == col
    diagonal = jnp.where(eye, block, 0.0)
    down = 1.0 / jnp.sum(diagonal, axis=1, keepdims=True)
    across = 1.0 / jnp.sum(diagonal, axis=0, keepdims=True)
    first = jnp.where(eye, 2.0 * down, 0.0) - down * block * across
    parts = split(first)
    inner = dot3(split(block), parts)
    return 2.0 * first - dot3(parts, split(inner))


def wrap(p):
    return lax.rem(p + 2 * NP, NP)


def among(value, choices):
    found = value == choices[0]
    for c in choices[1:]:
        found = found | (value == c)
    return found


ON = (
    {2: (0, 2, 4, 6, 8), -2: (0, 14), -1: (2, 4, 6, 8, 10), 1: (10, 12, 14)},
    {2: (0, 2, 4), -2: (0, 14, 12, 10), -1: (2, 4, 6, 8), 1: (8, 10, 12, 14)},
)


def edge0(step, p):
    places = sorted(set(ON[0][step]) | set(ON[1][step]))
    found = among(wrap(p), places)
    for k in range(1, PANELS):
        found = found | among(wrap(p - k), places)
    return found


def edge1(step, p):
    near = lax.rem(p, 4)
    if step == 4:
        return (near < PANELS) & (p < 8)
    if step == -4:
        return p < PANELS
    return near < PANELS


def kernel(
    x_ref,
    out_ref,
    rs,
    rows,
    hs,
    head,
    cols,
    fact,
    upper,
    ready0,
    ready1,
    sc_send,
    sc_recv,
    ra_send,
    ra_recv,
    hz_send,
    hz_recv,
    ha_send,
    ha_recv,
    z_send,
    z_recv,
    own_send,
    own_recv,
    zc_send,
    zc_recv,
    cc_send,
    cc_recv,
):
    p = lax.axis_index("prow")
    q = lax.axis_index("pcol")
    core = lax.rem(q, 2)
    chip = q // 2
    chip_y, chip_x = chip // SIDE, lax.rem(chip, SIDE)
    partner = q + 1 - 2 * core
    is_zero = core == 0
    is_one = core == 1
    is_root = p < PANELS
    scatters = (q == 0) | (q == 2)
    flows = chip > 0

    def remote(src, dst, send, recv, row, col):
        return pltpu.make_async_remote_copy(
            src_ref=src, dst_ref=dst, send_sem=send, recv_sem=recv, device_id=(row, col), device_id_type=MESH
        )

    def signal(sem, row, col):
        pl.semaphore_signal(sem, inc=1, device_id=(row, col), device_id_type=MESH)

    def count(flag):
        return flag.astype(jnp.int32)

    barrier = pltpu.get_barrier_semaphore()

    def greet(steps, edge):
        for s in steps:
            child, parent = wrap(p + s), wrap(p - s)

            @pl.when(edge(s, p) & (p < child))
            def _():
                signal(barrier, child, q)

            @pl.when(edge(s, parent) & (parent > p))
            def _():
                signal(barrier, parent, q)

    def greetings(steps, edge, twice=()):
        total = 0
        for s in steps:
            child, parent = wrap(p + s), wrap(p - s)
            total = total + count(edge(s, parent) & (parent < p)) + (1 + (s in twice)) * count(edge(s, p) & (child < p))
        return total

    def answer(steps, edge, ready):
        for i, s in enumerate(steps):
            parent = wrap(p - s)

            @pl.when(edge(s, parent) & (parent < p))
            def _():
                signal(ready.at[i], parent, q)

    def await_ready(steps, edge, ready, s):
        @pl.when(edge(s, p) & (p < wrap(p + s)))
        def _():
            pl.semaphore_wait(ready.at[steps.index(s)], 1)

    @pl.when(is_zero)
    def _():
        @pl.when(flows)
        def _():
            greet(STEPS0, edge0)

        @pl.when(scatters)
        def _():
            @pl.loop(0, NC)
            def _(j):
                signal(barrier, p, 2 * j + 1)

        @pl.when(jnp.logical_not(scatters))
        def _():
            signal(barrier, p, partner)

        pl.semaphore_wait(barrier, greetings(STEPS0, edge0, (1, -1)) * count(flows) + 1 + (NC - 1) * count(scatters))

        @pl.when(flows)
        def _():
            answer(STEPS0, edge0, ready0)

    @pl.when(is_one)
    def _():
        greet(STEPS1, edge1)

        for s in (1, -1):
            parent = wrap(p - s)

            @pl.when(flows & edge0(s, parent) & (parent > p))
            def _():
                signal(barrier, parent, partner)

        for step in (1, -1):
            signal(barrier, p, 2 * (chip_y * SIDE + lax.rem(chip_x + step + SIDE, SIDE)) + 1)
            signal(barrier, p, 2 * (lax.rem(chip_y + step + SIDE, SIDE) * SIDE + chip_x) + 1)

        for t in range(PANELS):

            @pl.when((partner != t) & (q != t))
            def _():
                signal(barrier, p, t)

        @pl.when(q == 1)
        def _():
            @pl.loop(1, NC)
            def _(j):
                signal(barrier, p, 2 * j + 1)

        signal(barrier, p, partner)
        others = 4 + 4 - count((partner == 0) | (partner == 2)) + (NC - 2) * count(q == 1)
        pl.semaphore_wait(barrier, greetings(STEPS1, edge1) + others)
        answer(STEPS1, edge1, ready1)

    def scatter(t):
        return remote(x_ref.at[:, :, t], rs.at[lax.rem(q, PANELS)], sc_send.at[t], sc_recv.at[lax.rem(q, PANELS)], p, 2 * t + 1)

    def each_scatter(act):
        @pl.when(q < PANELS)
        def _():
            @pl.loop(0, NC)
            def _(t):
                @pl.when(2 * t + 1 != q)
                def _():
                    act(scatter(t))

    def own(half):
        piece = cols.at[1, lax.rem(p, PANELS), half]
        return remote(x_ref.at[0, half], piece, own_send.at[half], own_recv.at[half], p, partner)

    @pl.when(is_one & is_root & flows)
    def _():
        own(0).start()
        own(1).start()

    each_scatter(lambda copy: copy.start())

    def col_piece(k, i):
        half, j = i // 4, lax.rem(i, 4)
        return cols.at[j // 2, k, half, pl.ds(lax.rem(j, 2) * (CR // S), CR // S)]

    def col_copy(k, i, step):
        piece = col_piece(k, i)
        n = STEPS0.index(step)
        to = q + lax.rem(i, 4) // 2 if step in (1, -1) else q
        return remote(piece, piece, z_send.at[n, k * CHUNKS + i], z_recv.at[k * CHUNKS + i], wrap(p + step), to)

    def to_one(k, i):
        piece = col_piece(k, i)
        return remote(piece, piece, zc_send.at[k], zc_recv.at[k], p, partner)

    def pass_on(k, i, act):
        away = wrap(p - k)
        for half in range(2):

            @pl.when(i // 4 == half)
            def _():
                for s in STEPS0:

                    @pl.when(among(away, ON[half][s]))
                    def _():
                        act(col_copy(k, i, s))

    def in_turn(k, i):
        away = wrap(p - k)
        return lax.rem(i + 4 * count(away > 8), CHUNKS)

    @pl.when(is_zero & flows)
    def _():
        mine = lax.rem(p, PANELS)

        def start_own(n, step):
            first = 0 if step == 2 else 4

            @pl.when(is_root & (n < CHUNKS))
            def _():
                @pl.when(n >= WINDOW)
                def _():
                    col_copy(mine, lax.rem(n - WINDOW + first, CHUNKS), step).wait_send()

                col_copy(mine, lax.rem(n + first, CHUNKS), step).start()

        @pl.when(is_root)
        def _():
            cols[0, mine] = x_ref[0]

        await_ready(STEPS0, edge0, ready0, 2)

        @pl.loop(0, CHUNKS + LAG)
        def _(n):
            for half, turn in ((0, 2), (1, LAG + 2)):

                @pl.when(is_root & (n == turn))
                def _():
                    own(half).wait_recv()

            start_own(n, 2)

            @pl.when(n == LAG)
            def _():
                for s in (-2, -1, 1):
                    await_ready(STEPS0, edge0, ready0, s)

            @pl.when(n >= LAG)
            def _():
                i = n - LAG
                start_own(i, -2)
                for k in reversed(range(PANELS)):
                    away = wrap(p - k)

                    @pl.when((lax.rem(away, 2) == 0) & (away != 0))
                    def _():
                        t = in_turn(k, i)
                        col_copy(k, t, 2).wait_recv()
                        pass_on(k, t, lambda copy: copy.start())

                        @pl.when(lax.rem(t, 4) >= 2)
                        def _():
                            to_one(k, t).start()

        @pl.when(is_root)
        def _():
            @pl.loop(CHUNKS - WINDOW, CHUNKS)
            def _(n):
                col_copy(mine, n, 2).wait_send()
                col_copy(mine, lax.rem(n + 4, CHUNKS), -2).wait_send()

    def await_fills():
        @pl.when(flows)
        def _():
            for k in range(PANELS):

                @pl.when(lax.rem(wrap(p - k), 2) == 1)
                def _():
                    @pl.loop(0, CHUNKS // 2)
                    def _(i):
                        col_copy(k, (i // 2) * 4 + core * 2 + lax.rem(i, 2), 2).wait_recv()

                @pl.when(is_one & (p != k) & (lax.rem(wrap(p - k), 2) == 0))
                def _():
                    remote(cols.at[1, k], cols.at[1, k], zc_send.at[k], zc_recv.at[k], p, partner).wait_recv()

    @pl.when(jnp.logical_not(flows))
    def _():
        cols[...] = jnp.zeros_like(cols)

    def across(buffer, n, half, c):
        piece = buffer.at[half, c]
        return remote(piece, piece, cc_send.at[n], cc_recv.at[n], p, partner)

    def whole(buffer, n):
        return remote(buffer, buffer, cc_send.at[n], cc_recv.at[n], p, partner)

    class Ring:
        def __init__(self, buffer, send, recv, n):
            self.buffer, self.send, self.recv, self.n = buffer, send, recv, n

        def line(self, stage, half, t, step):
            if stage == half:
                x = lax.rem(chip_x + step + SIDE, SIDE)
                return (chip_y if stage == 0 else t) * SIDE + x
            y = lax.rem(chip_y + step + SIDE, SIDE)
            return y * SIDE + (chip_x if stage == 0 else t)

        def neighbour(self, stage, half, step):
            if stage == half:
                return 2 * (chip_y * SIDE + lax.rem(chip_x + step + SIDE, SIDE)) + 1
            return 2 * (lax.rem(chip_y + step + SIDE, SIDE) * SIDE + chip_x) + 1

        def copy(self, stage, half, t, kind):
            step = 1 if kind in (0, 2) else -1
            piece = self.buffer.at[half, self.line(stage, half, t, 0 if kind < 2 else -step)]
            if kind >= 2:
                piece = piece.at[:, :, :, pl.ds((kind - 2) * (B // 2), B // 2)]
            i = (stage * SIDE + t) * 2 + half
            return remote(piece, piece, self.send.at[kind, i], self.recv.at[kind, i], p, self.neighbour(stage, half, step))

        def each(self, stage, act):
            if stage == 0:
                for half in range(2):
                    act(half, 0)
                return

            @pl.loop(0, SIDE)
            def _(t):
                for half in range(2):
                    act(half, t)

        def push(self, stage, half, t, step):
            if stage == 1:
                across(self.buffer, self.n, half, self.line(stage, half, t, step)).start()

        def begin(self, stage):
            def act(half, t):
                self.copy(stage, half, t, 0).start()
                self.copy(stage, half, t, 1).start()
                self.push(stage, half, t, 0)

            self.each(stage, act)

        def middle(self, stage):
            def act(half, t):
                for kind in range(2):
                    self.copy(stage, half, t, kind).wait_recv()
                    self.copy(stage, half, t, 2 + kind).start()
                    self.push(stage, half, t, -1 if kind == 0 else 1)

            self.each(stage, act)

        def end(self, stage):
            def act(half, t):
                for kind in (2, 3):
                    self.copy(stage, half, t, kind).wait_recv()
                self.push(stage, half, t, 2)

            self.each(stage, act)

        def sent(self):
            for stage in range(2):

                def act(half, t):
                    for kind in range(4):
                        self.copy(stage, half, t, kind).wait_send()

                self.each(stage, act)

    near = lax.rem(p, 4)
    mine4 = lax.rem(near, PANELS)
    anchor = near < PANELS

    def along(step):
        n = STEPS1.index(step)
        return remote(hs.at[mine4], hs.at[mine4], hz_send.at[n], hz_recv.at[mine4], wrap(p + step), q)

    row_ring = Ring(rows, ra_send, ra_recv, 0)
    head_ring = Ring(head, ha_send, ha_recv, 1)

    @pl.when(is_one)
    def _():
        @pl.when(q == 1)
        def _():
            rs[1] = x_ref[:, :, 0]

        for k in range(PANELS):

            @pl.when(q != k)
            def _():
                remote(x_ref.at[:, :, 0], rs.at[k], sc_send.at[0], sc_recv.at[k], p, partner).wait_recv()

        @pl.when(is_root)
        def _():
            hs[mine4] = rs[:, 0]

        @pl.when(anchor & jnp.logical_not(is_root))
        def _():
            along(4).wait_recv()

        for s in STEPS1:
            await_ready(STEPS1, edge1, ready1, s)

            @pl.when(edge1(s, p))
            def _():
                along(s).start()

        for half in range(2):
            rows[half, chip] = rs[:, :, half]
        row_ring.begin(0)
        row_ring.middle(0)

        for k in range(PANELS):

            @pl.when(near != k)
            def _():
                remote(hs.at[k], hs.at[k], hz_send.at[0], hz_recv.at[k], p, partner).wait_recv()

        for half in range(2):
            head[half, chip] = hs[:, :, half]
        head_ring.begin(0)
        row_ring.end(0)
        row_ring.begin(1)
        head_ring.middle(0)
        row_ring.middle(1)
        head_ring.end(0)
        head_ring.begin(1)

        @pl.when(is_root & flows)
        def _():
            cols[1, lax.rem(p, PANELS)] = x_ref[0]

        row_ring.end(1)
        head_ring.middle(1)
        head_ring.end(1)

    @pl.when(is_zero)
    def _():
        whole(head, 1).wait_recv()

    def block(i, j):
        return head[:, :, i, j].reshape(B, B)

    a = {(i, j): block(i, j) for i in range(PANELS) for j in range(PANELS)}
    halves = {}
    for k in range(PANELS):
        inverse = invert(a[k, k])
        fact[k, k] = inverse
        halves[k, k] = split(inverse)
        for j in range(k + 1, PANELS):
            fact[k, j] = a[k, j]
            halves[k, j] = split(a[k, j])
        for i in range(k + 1, PANELS):
            factor = dot3(split(a[i, k]), halves[k, k])
            fact[i, k] = factor
            halves[i, k] = split(factor)
            for j in range(k + 1, PANELS):
                a[i, j] = a[i, j] - dot3(halves[i, k], halves[k, j])

    await_fills()
    is_panel = q < PANELS
    eye = (
        lax.broadcasted_iota(jnp.int32, (B, B), 0) == lax.broadcasted_iota(jnp.int32, (B, B), 1)
    ).astype(jnp.float32)
    y = []
    for i in range(PANELS):
        value = cols[core, i].reshape(B, B)
        for k in range(i):
            value = value - dot3(halves[i, k], y[k])
        upper[i] = value
        y.append(split(value))

    right = [None] * PANELS
    for i in reversed(range(PANELS)):
        value = jnp.where(is_panel, jnp.where(q == i, eye, 0.0), upper[i])
        for k in range(i + 1, PANELS):
            value = value - dot3(halves[i, k], right[k])
        right[i] = split(dot3(halves[i, i], split(value)))

    @pl.when(is_zero)
    def _():
        whole(rows, 0).wait_recv()

    keep = jnp.where(is_panel, 0.0, 1.0)
    sign = jnp.where(is_panel, 1.0, -1.0)
    for b in range(2):
        total = jnp.zeros((B, B), jnp.float32)
        for k in range(PANELS):
            total = total + dot3(split(rows[:, :, k, b].reshape(B, B)), right[k])
        out_ref[b] = keep * x_ref[b].reshape(B, B) + sign * total

    @pl.when(is_root & is_panel)
    def _():
        out_ref[0] = fact[lax.rem(p, PANELS), lax.rem(q, PANELS)]

    @pl.when(is_root & (q >= PANELS))
    def _():
        out_ref[0] = upper[lax.rem(p, PANELS)]

    each_scatter(lambda copy: copy.wait_send())

    @pl.when(is_zero & flows)
    def _():
        @pl.loop(0, CHUNKS)
        def _(i):
            for k in range(PANELS):

                @pl.when(p != k)
                def _():
                    pass_on(k, i, lambda copy: copy.wait_send())

        for k in range(PANELS):

            @pl.when((p != k) & (lax.rem(wrap(p - k), 2) == 0))
            def _():
                remote(cols.at[1, k], cols.at[1, k], zc_send.at[k], zc_recv.at[k], p, partner).wait_send()

    @pl.when(is_one)
    def _():
        @pl.when(is_root & flows)
        def _():
            own(0).wait_send()
            own(1).wait_send()

        for s in STEPS1:

            @pl.when(edge1(s, p))
            def _():
                along(s).wait_send()

        row_ring.sent()
        head_ring.sent()
        whole(rows, 0).wait_send()
        whole(head, 1).wait_send()


def body(matrix):
    shape = matrix.shape
    f32 = jnp.float32
    dma = pltpu.SemaphoreType.DMA
    out = pl.pallas_call(
        kernel,
        out_shape=jax.ShapeDtypeStruct((2, B, B), f32),
        in_specs=[pl.BlockSpec(memory_space=pltpu.VMEM)],
        out_specs=pl.BlockSpec(memory_space=pltpu.VMEM),
        scratch_shapes=[
            pltpu.VMEM((PANELS, 2, 2, S, B), f32),
            pltpu.VMEM((2, NC, PANELS, 2, S, B), f32),
            pltpu.VMEM((PANELS, PANELS, 2, S, B), f32),
            pltpu.VMEM((2, NC, PANELS, PANELS, S, B), f32),
            pltpu.VMEM((2, PANELS, 2, NC, S, B), f32),
            pltpu.VMEM((PANELS, PANELS, B, B), f32),
            pltpu.VMEM((PANELS, B, B), f32),
            pltpu.SemaphoreType.REGULAR((len(STEPS0),)),
            pltpu.SemaphoreType.REGULAR((len(STEPS1),)),
            dma((NC,)),
            dma((PANELS,)),
            dma((4, 4 * SIDE)),
            dma((4, 4 * SIDE)),
            dma((len(STEPS1),)),
            dma((PANELS,)),
            dma((4, 4 * SIDE)),
            dma((4, 4 * SIDE)),
            dma((len(STEPS0), PANELS * CHUNKS)),
            dma((PANELS * CHUNKS,)),
            dma((2,)),
            dma((2,)),
            dma((PANELS,)),
            dma((PANELS,)),
            dma((2,)),
            dma((2,)),
        ],
        compiler_params=pltpu.CompilerParams(
            collective_id=0, has_side_effects=True, vmem_limit_bytes=48 * 1024 * 1024
        ),
    )(matrix.reshape(2, 2, NC, S, B))
    return out.reshape(shape)


def solution(mesh):
    spec = P(None, "prow", None, "pcol", None)
    return jax.shard_map(body, mesh=mesh, in_specs=(spec,), out_specs=spec, check_vma=False)
```

```python
import functools

import jax
import jax.numpy as jnp
from jax import lax
from jax.experimental import pallas as pl
from jax.experimental.pallas import tpu as pltpu
from jax.sharding import PartitionSpec as P

B = 256
PANELS = 3
NP = 16
NQ = 32
NC = NQ // 2
S = B // NC // 2
SIDE = 4
CHUNKS = 8
CR = 2 * B // CHUNKS
WINDOW = 2
LAG = 3
MESH = pl.DeviceIdType.MESH
STEPS0 = (2, 1, -1, -2)
STEPS1 = (4, 1, -1, -2, -4)


def split(value):
    high = value.astype(jnp.bfloat16)
    return high, (value - high.astype(jnp.float32)).astype(jnp.bfloat16)


def products(lefts, right):
    dot = functools.partial(jnp.dot, preferred_element_type=jnp.float32)
    return [dot(left[0], right[0]) + (dot(left[0], right[1]) + dot(left[1], right[0])) for left in lefts]


def product(left, right):
    return products([left], right)[0]


def invert(block):
    row = lax.broadcasted_iota(jnp.int32, (B, B), 0)
    col = lax.broadcasted_iota(jnp.int32, (B, B), 1)
    eye = row == col
    diagonal = jnp.where(eye, block, 0.0)
    down = 1.0 / jnp.sum(diagonal, axis=1, keepdims=True)
    across = 1.0 / jnp.sum(diagonal, axis=0, keepdims=True)
    first = jnp.where(eye, 2.0 * down, 0.0) - down * block * across
    parts = split(first)
    inner = product(split(block), parts)
    return 2.0 * first - product(parts, split(inner))


def wrap(p):
    return lax.rem(p + 2 * NP, NP)


def among(value, choices):
    found = value == choices[0]
    for c in choices[1:]:
        found = found | (value == c)
    return found


ON = (
    {2: (0, 2, 4, 6, 8), -2: (0, 14), -1: (2, 4, 6, 8, 10), 1: (10, 12, 14)},
    {2: (0, 2, 4), -2: (0, 14, 12, 10), -1: (2, 4, 6, 8), 1: (8, 10, 12, 14)},
)


def edge0(step, p):
    places = sorted(set(ON[0][step]) | set(ON[1][step]))
    found = among(wrap(p), places)
    for k in range(1, PANELS):
        found = found | among(wrap(p - k), places)
    return found


def edge1(step, p):
    near = lax.rem(p, 4)
    if step == 4:
        return (near < PANELS) & (p < 8)
    if step == -4:
        return p < PANELS
    return near < PANELS


def kernel(
    x_ref,
    out_ref,
    rs,
    rows,
    hs,
    head,
    cols,
    fact,
    upper,
    ready0,
    ready1,
    sc_send,
    sc_recv,
    ra_send,
    ra_recv,
    hz_send,
    hz_recv,
    ha_send,
    ha_recv,
    z_send,
    z_recv,
    own_send,
    own_recv,
    zc_send,
    zc_recv,
    cc_send,
    cc_recv,
):
    p = lax.axis_index("prow")
    q = lax.axis_index("pcol")
    core = lax.rem(q, 2)
    chip = q // 2
    chip_y, chip_x = chip // SIDE, lax.rem(chip, SIDE)
    partner = q + 1 - 2 * core
    is_zero = core == 0
    is_one = core == 1
    is_root = p < PANELS
    scatters = (q == 0) | (q == 2)
    flows = chip > 0

    def remote(src, dst, send, recv, row, col):
        return pltpu.make_async_remote_copy(
            src_ref=src, dst_ref=dst, send_sem=send, recv_sem=recv, device_id=(row, col), device_id_type=MESH
        )

    def signal(sem, row, col):
        pl.semaphore_signal(sem, inc=1, device_id=(row, col), device_id_type=MESH)

    def count(flag):
        return flag.astype(jnp.int32)

    barrier = pltpu.get_barrier_semaphore()

    def greet(steps, edge):
        for s in steps:
            child, parent = wrap(p + s), wrap(p - s)

            @pl.when(edge(s, p) & (p < child))
            def _():
                signal(barrier, child, q)

            @pl.when(edge(s, parent) & (parent > p))
            def _():
                signal(barrier, parent, q)

    def greetings(steps, edge, twice=()):
        total = 0
        for s in steps:
            child, parent = wrap(p + s), wrap(p - s)
            total = total + count(edge(s, parent) & (parent < p)) + (1 + (s in twice)) * count(edge(s, p) & (child < p))
        return total

    def answer(steps, edge, ready):
        for i, s in enumerate(steps):
            parent = wrap(p - s)

            @pl.when(edge(s, parent) & (parent < p))
            def _():
                signal(ready.at[i], parent, q)

    def await_ready(steps, edge, ready, s):
        @pl.when(edge(s, p) & (p < wrap(p + s)))
        def _():
            pl.semaphore_wait(ready.at[steps.index(s)], 1)

    @pl.when(is_zero)
    def _():
        @pl.when(flows)
        def _():
            greet(STEPS0, edge0)

        @pl.when(scatters)
        def _():
            @pl.loop(0, NC)
            def _(j):
                signal(barrier, p, 2 * j + 1)

        @pl.when(jnp.logical_not(scatters))
        def _():
            signal(barrier, p, partner)

        pl.semaphore_wait(barrier, greetings(STEPS0, edge0, (1, -1)) * count(flows) + 1 + (NC - 1) * count(scatters))

        @pl.when(flows)
        def _():
            answer(STEPS0, edge0, ready0)

    @pl.when(is_one)
    def _():
        greet(STEPS1, edge1)

        for s in (1, -1):
            parent = wrap(p - s)

            @pl.when(flows & edge0(s, parent) & (parent > p))
            def _():
                signal(barrier, parent, partner)

        for step in (1, -1):
            signal(barrier, p, 2 * (chip_y * SIDE + lax.rem(chip_x + step + SIDE, SIDE)) + 1)
            signal(barrier, p, 2 * (lax.rem(chip_y + step + SIDE, SIDE) * SIDE + chip_x) + 1)

        for t in range(PANELS):

            @pl.when((partner != t) & (q != t))
            def _():
                signal(barrier, p, t)

        @pl.when(q == 1)
        def _():
            @pl.loop(1, NC)
            def _(j):
                signal(barrier, p, 2 * j + 1)

        signal(barrier, p, partner)
        others = 4 + 4 - count((partner == 0) | (partner == 2)) + (NC - 2) * count(q == 1)
        pl.semaphore_wait(barrier, greetings(STEPS1, edge1) + others)
        answer(STEPS1, edge1, ready1)

    def scatter(t, b):
        k = lax.rem(q, PANELS)
        return remote(x_ref.at[b, :, t], rs.at[k, b], sc_send.at[b, t], sc_recv.at[b, k], p, 2 * t + 1)

    def each_scatter(act):
        @pl.when(q < PANELS)
        def _():
            for b in range(2):

                @pl.loop(0, NC)
                def _(t):
                    @pl.when(2 * t + 1 != q)
                    def _():
                        act(scatter(t, b))

    def own(half):
        piece = cols.at[1, lax.rem(p, PANELS), half]
        return remote(x_ref.at[0, half], piece, own_send.at[half], own_recv.at[half], p, partner)

    @pl.when(is_one & is_root & flows)
    def _():
        own(0).start()
        own(1).start()

    each_scatter(lambda copy: copy.start())

    def col_piece(k, i):
        half, j = i // 4, lax.rem(i, 4)
        return cols.at[j // 2, k, half, pl.ds(lax.rem(j, 2) * (CR // S), CR // S)]

    def col_copy(k, i, step):
        piece = col_piece(k, i)
        n = STEPS0.index(step)
        to = q + lax.rem(i, 4) // 2 if step in (1, -1) else q
        return remote(piece, piece, z_send.at[n, k * CHUNKS + i], z_recv.at[k * CHUNKS + i], wrap(p + step), to)

    def to_one(k, i):
        piece = col_piece(k, i)
        return remote(piece, piece, zc_send.at[k], zc_recv.at[k], p, partner)

    def live(i):
        return (chip > 1) | (lax.rem(i, 4) >= 2)

    def pass_on(k, i, act):
        away = wrap(p - k)
        for half in range(2):

            @pl.when(i // 4 == half)
            def _():
                for s in STEPS0:

                    @pl.when(among(away, ON[half][s]))
                    def _():
                        act(col_copy(k, i, s))

    def in_turn(k, i):
        away = wrap(p - k)
        return lax.rem(i + 4 * count(away > 8), CHUNKS)

    def wait_passed(first, last):
        @pl.loop(first, last)
        def _(i):
            @pl.when(live(i))
            def _():
                for k in range(PANELS):

                    @pl.when(p != k)
                    def _():
                        pass_on(k, in_turn(k, i), lambda copy: copy.wait_send())

    @pl.when(is_zero & flows)
    def _():
        mine = lax.rem(p, PANELS)

        def start_own(n, step):
            first = 0 if step == 2 else 4

            @pl.when(is_root & (n < CHUNKS) & live(n))
            def _():
                @pl.when((n >= WINDOW) & live(n + CHUNKS - WINDOW))
                def _():
                    col_copy(mine, lax.rem(n - WINDOW + first, CHUNKS), step).wait_send()

                col_copy(mine, lax.rem(n + first, CHUNKS), step).start()

        @pl.when(is_root)
        def _():
            cols[0, mine] = x_ref[0]

        await_ready(STEPS0, edge0, ready0, 2)

        @pl.loop(0, CHUNKS + LAG)
        def _(n):
            for half, turn in ((0, 2), (1, LAG + 2)):

                @pl.when(is_root & (n == turn))
                def _():
                    own(half).wait_recv()

            start_own(n, 2)

            @pl.when(n == LAG)
            def _():
                for s in (-2, -1, 1):
                    await_ready(STEPS0, edge0, ready0, s)

            @pl.when(n >= LAG)
            def _():
                i = n - LAG
                start_own(i, -2)
                for k in reversed(range(PANELS)):
                    away = wrap(p - k)

                    @pl.when((lax.rem(away, 2) == 0) & (away != 0) & live(i))
                    def _():
                        t = in_turn(k, i)
                        col_copy(k, t, 2).wait_recv()
                        pass_on(k, t, lambda copy: copy.start())

                        @pl.when(lax.rem(t, 4) >= 2)
                        def _():
                            to_one(k, t).start()

        wait_passed(0, CHUNKS - 3)

    def await_fills():
        @pl.when(flows)
        def _():
            for k in range(PANELS):

                @pl.when((lax.rem(wrap(p - k), 2) == 1) & (is_one | (chip > 1)))
                def _():
                    @pl.loop(0, CHUNKS // 2)
                    def _(i):
                        col_copy(k, (i // 2) * 4 + core * 2 + lax.rem(i, 2), 2).wait_recv()

                @pl.when(is_one & (p != k) & (lax.rem(wrap(p - k), 2) == 0))
                def _():
                    remote(cols.at[1, k], cols.at[1, k], zc_send.at[k], zc_recv.at[k], p, partner).wait_recv()

    @pl.when((chip == 0) | ((chip == 1) & is_zero))
    def _():
        cols[core] = jnp.zeros_like(cols[core])

    def across(buffer, n, half, c):
        piece = buffer.at[half, c]
        return remote(piece, piece, cc_send.at[n], cc_recv.at[n], p, partner)

    def whole(buffer, n):
        return remote(buffer, buffer, cc_send.at[n], cc_recv.at[n], p, partner)

    class Ring:
        def __init__(self, buffer, send, recv, n):
            self.buffer, self.send, self.recv, self.n = buffer, send, recv, n

        def line(self, stage, half, t, step):
            if stage == half:
                x = lax.rem(chip_x + step + SIDE, SIDE)
                return (chip_y if stage == 0 else t) * SIDE + x
            y = lax.rem(chip_y + step + SIDE, SIDE)
            return y * SIDE + (chip_x if stage == 0 else t)

        def neighbour(self, stage, half, step):
            if stage == half:
                return 2 * (chip_y * SIDE + lax.rem(chip_x + step + SIDE, SIDE)) + 1
            return 2 * (lax.rem(chip_y + step + SIDE, SIDE) * SIDE + chip_x) + 1

        def copy(self, stage, half, t, kind):
            step = 1 if kind in (0, 2) else -1
            piece = self.buffer.at[half, self.line(stage, half, t, 0 if kind < 2 else -step)]
            if kind >= 2:
                piece = piece.at[:, :, :, pl.ds((kind - 2) * (B // 2), B // 2)]
            i = (stage * SIDE + t) * 2 + half
            return remote(piece, piece, self.send.at[kind, i], self.recv.at[kind, i], p, self.neighbour(stage, half, step))

        def each(self, stage, act):
            if stage == 0:
                for half in range(2):
                    act(half, 0)
                return

            @pl.loop(0, SIDE)
            def _(t):
                for half in range(2):
                    act(half, t)

        def push(self, stage, half, t, step):
            if stage == 1:
                across(self.buffer, self.n, half, self.line(stage, half, t, step)).start()

        def begin(self, stage):
            def act(half, t):
                self.copy(stage, half, t, 0).start()
                self.copy(stage, half, t, 1).start()
                self.push(stage, half, t, 0)

            self.each(stage, act)

        def middle(self, stage):
            def act(half, t):
                for kind in range(2):
                    self.copy(stage, half, t, kind).wait_recv()
                    self.copy(stage, half, t, 2 + kind).start()
                    self.push(stage, half, t, -1 if kind == 0 else 1)

            self.each(stage, act)

        def end(self, stage):
            def act(half, t):
                for kind in (2, 3):
                    self.copy(stage, half, t, kind).wait_recv()
                self.push(stage, half, t, 2)

            self.each(stage, act)

        def sent(self):
            for stage in range(2):

                def act(half, t):
                    for kind in range(4):
                        self.copy(stage, half, t, kind).wait_send()

                self.each(stage, act)

    near = lax.rem(p, 4)
    mine4 = lax.rem(near, PANELS)
    anchor = near < PANELS

    def along(step):
        n = STEPS1.index(step)
        return remote(hs.at[mine4], hs.at[mine4], hz_send.at[n], hz_recv.at[mine4], wrap(p + step), q)

    row_ring = Ring(rows, ra_send, ra_recv, 0)
    head_ring = Ring(head, ha_send, ha_recv, 1)

    @pl.when(is_one)
    def _():
        @pl.when(q == 1)
        def _():
            rs[1] = x_ref[:, :, 0]

        def scattered(b):
            for k in range(PANELS):

                @pl.when(q != k)
                def _():
                    remote(x_ref.at[b, :, 0], rs.at[k, b], sc_send.at[b, 0], sc_recv.at[b, k], p, partner).wait_recv()

        @pl.when(is_root)
        def _():
            scattered(0)
            hs[mine4] = rs[:, 0]

        @pl.when(anchor & jnp.logical_not(is_root))
        def _():
            along(4).wait_recv()

        for s in STEPS1:
            await_ready(STEPS1, edge1, ready1, s)

            @pl.when(edge1(s, p))
            def _():
                along(s).start()

        @pl.when(jnp.logical_not(is_root))
        def _():
            scattered(0)

        scattered(1)
        for half in range(2):
            rows[half, chip] = rs[:, :, half]
        row_ring.begin(0)

        for k in range(PANELS):

            @pl.when(near != k)
            def _():
                remote(hs.at[k], hs.at[k], hz_send.at[0], hz_recv.at[k], p, partner).wait_recv()

        for half in range(2):
            head[half, chip] = hs[:, :, half]
        head_ring.begin(0)
        head_ring.middle(0)
        head_ring.end(0)
        head_ring.begin(1)
        row_ring.middle(0)

        @pl.when(is_root & flows)
        def _():
            cols[1, lax.rem(p, PANELS)] = x_ref[0]

        head_ring.middle(1)
        row_ring.end(0)
        row_ring.begin(1)
        head_ring.end(1)

    @pl.when(is_zero)
    def _():
        whole(head, 1).wait_recv()

    def block(i, j):
        return head[:, :, i, j].reshape(B, B)

    a = {(i, j): block(i, j) for i in range(PANELS) for j in range(PANELS)}
    halves = {}
    for k in range(PANELS):
        inverse = invert(a[k, k])
        fact[k, k] = inverse
        halves[k, k] = split(inverse)
        below = range(k + 1, PANELS)
        if below:
            for i, factor in zip(below, products([split(a[i, k]) for i in below], halves[k, k])):
                fact[i, k] = factor
                halves[i, k] = split(factor)
        for j in below:
            fact[k, j] = a[k, j]
            halves[k, j] = split(a[k, j])
            for i, update in zip(below, products([halves[i, k] for i in below], halves[k, j])):
                a[i, j] = a[i, j] - update
        if k == 1:

            @pl.when(is_one)
            def _():
                row_ring.middle(1)

    await_fills()
    is_panel = q < PANELS
    eye = (
        lax.broadcasted_iota(jnp.int32, (B, B), 0) == lax.broadcasted_iota(jnp.int32, (B, B), 1)
    ).astype(jnp.float32)
    value = [cols[core, i].reshape(B, B) for i in range(PANELS)]
    for i in range(PANELS):
        upper[i] = value[i]
        later = range(i + 1, PANELS)
        if later:
            for m, update in zip(later, products([halves[m, i] for m in later], split(value[i]))):
                value[m] = value[m] - update

    right = [None] * PANELS
    value = [jnp.where(is_panel, jnp.where(q == i, eye, 0.0), upper[i]) for i in range(PANELS)]
    for i in reversed(range(PANELS)):
        right[i] = split(product(halves[i, i], split(value[i])))
        if i:
            for m, update in zip(range(i), products([halves[m, i] for m in range(i)], right[i])):
                value[m] = value[m] - update

    @pl.when(is_one)
    def _():
        row_ring.end(1)

    @pl.when(is_zero)
    def _():
        whole(rows, 0).wait_recv()

    keep = jnp.where(is_panel, 0.0, 1.0)
    sign = jnp.where(is_panel, 1.0, -1.0)
    total = [None, None]
    for k in range(PANELS):
        panel = [split(rows[:, :, k, b].reshape(B, B)) for b in range(2)]
        for b, term in enumerate(products(panel, right[k])):
            total[b] = term if k == 0 else total[b] + term
    for b in range(2):
        out_ref[b] = keep * x_ref[b].reshape(B, B) + sign * total[b]

    @pl.when(is_root & is_panel)
    def _():
        out_ref[0] = fact[lax.rem(p, PANELS), lax.rem(q, PANELS)]

    @pl.when(is_root & (q >= PANELS))
    def _():
        out_ref[0] = upper[lax.rem(p, PANELS)]

    each_scatter(lambda copy: copy.wait_send())

    @pl.when(is_zero & flows)
    def _():
        @pl.when(is_root)
        def _():
            mine = lax.rem(p, PANELS)

            @pl.loop(0, CHUNKS)
            def _(n):
                @pl.when(live(n) & ((n >= CHUNKS - WINDOW) | jnp.logical_not(live(n + WINDOW))))
                def _():
                    col_copy(mine, n, 2).wait_send()
                    col_copy(mine, lax.rem(n + 4, CHUNKS), -2).wait_send()

        wait_passed(CHUNKS - 3, CHUNKS)
        for k in range(PANELS):

            @pl.when((p != k) & (lax.rem(wrap(p - k), 2) == 0))
            def _():
                remote(cols.at[1, k], cols.at[1, k], zc_send.at[k], zc_recv.at[k], p, partner).wait_send()

    @pl.when(is_one)
    def _():
        @pl.when(is_root & flows)
        def _():
            own(0).wait_send()
            own(1).wait_send()

        for s in STEPS1:

            @pl.when(edge1(s, p))
            def _():
                along(s).wait_send()

        row_ring.sent()
        head_ring.sent()
        whole(rows, 0).wait_send()
        whole(head, 1).wait_send()


def body(matrix):
    shape = matrix.shape
    f32 = jnp.float32
    dma = pltpu.SemaphoreType.DMA
    out = pl.pallas_call(
        kernel,
        out_shape=jax.ShapeDtypeStruct((2, B, B), f32),
        in_specs=[pl.BlockSpec(memory_space=pltpu.VMEM)],
        out_specs=pl.BlockSpec(memory_space=pltpu.VMEM),
        scratch_shapes=[
            pltpu.VMEM((PANELS, 2, 2, S, B), f32),
            pltpu.VMEM((2, NC, PANELS, 2, S, B), f32),
            pltpu.VMEM((PANELS, PANELS, 2, S, B), f32),
            pltpu.VMEM((2, NC, PANELS, PANELS, S, B), f32),
            pltpu.VMEM((2, PANELS, 2, NC, S, B), f32),
            pltpu.VMEM((PANELS, PANELS, B, B), f32),
            pltpu.VMEM((PANELS, B, B), f32),
            pltpu.SemaphoreType.REGULAR((len(STEPS0),)),
            pltpu.SemaphoreType.REGULAR((len(STEPS1),)),
            dma((2, NC)),
            dma((2, PANELS)),
            dma((4, 4 * SIDE)),
            dma((4, 4 * SIDE)),
            dma((len(STEPS1),)),
            dma((PANELS,)),
            dma((4, 4 * SIDE)),
            dma((4, 4 * SIDE)),
            dma((len(STEPS0), PANELS * CHUNKS)),
            dma((PANELS * CHUNKS,)),
            dma((2,)),
            dma((2,)),
            dma((PANELS,)),
            dma((PANELS,)),
            dma((2,)),
            dma((2,)),
        ],
        compiler_params=pltpu.CompilerParams(
            collective_id=0, has_side_effects=True, vmem_limit_bytes=48 * 1024 * 1024
        ),
    )(matrix.reshape(2, 2, NC, S, B))
    return out.reshape(shape)


def solution(mesh):
    spec = P(None, "prow", None, "pcol", None)
    return jax.shard_map(body, mesh=mesh, in_specs=(spec,), out_specs=spec, check_vma=False)
```

```python
import functools

import jax
import jax.numpy as jnp
from jax import lax
from jax.experimental import pallas as pl
from jax.experimental.pallas import tpu as pltpu
from jax.sharding import PartitionSpec as P

B = 256
PANELS = 3
NP = 16
NQ = 32
NC = NQ // 2
S = B // NC // 2
SIDE = 4
CHUNKS = 8
CR = 2 * B // CHUNKS
WINDOW = 2
LAG = 3
MESH = pl.DeviceIdType.MESH
STEPS0 = (2, 1, -1, -2)
STEPS1 = (4, 1, -1, -2, -4)


def split(value):
    high = value.astype(jnp.bfloat16)
    return high, (value - high.astype(jnp.float32)).astype(jnp.bfloat16)


def products(lefts, right):
    dot = functools.partial(jnp.dot, preferred_element_type=jnp.float32)
    return [dot(left[0], right[0]) + (dot(left[0], right[1]) + dot(left[1], right[0])) for left in lefts]


def product(left, right):
    return products([left], right)[0]


def invert(block):
    row = lax.broadcasted_iota(jnp.int32, (B, B), 0)
    col = lax.broadcasted_iota(jnp.int32, (B, B), 1)
    eye = row == col
    diagonal = jnp.where(eye, block, 0.0)
    down = 1.0 / jnp.sum(diagonal, axis=1, keepdims=True)
    across = 1.0 / jnp.sum(diagonal, axis=0, keepdims=True)
    first = jnp.where(eye, 2.0 * down, 0.0) - down * block * across
    parts = split(first)
    inner = product(split(block), parts)
    return 2.0 * first - product(parts, split(inner))


def wrap(p):
    return lax.rem(p + 2 * NP, NP)


def among(value, choices):
    found = value == choices[0]
    for c in choices[1:]:
        found = found | (value == c)
    return found


ON = (
    {2: (0, 2, 4, 6, 8), -2: (0, 14), -1: (2, 4, 6, 8, 10), 1: (10, 12, 14)},
    {2: (0, 2, 4), -2: (0, 14, 12, 10), -1: (2, 4, 6, 8), 1: (8, 10, 12, 14)},
)


def edge0(step, p):
    places = sorted(set(ON[0][step]) | set(ON[1][step]))
    found = among(wrap(p), places)
    for k in range(1, PANELS):
        found = found | among(wrap(p - k), places)
    return found


def edge1(step, p):
    near = lax.rem(p, 4)
    if step == 4:
        return (near < PANELS) & (p < 8)
    if step == -4:
        return p < PANELS
    return near < PANELS


def kernel(
    x_hbm,
    out_hbm,
    x_ref,
    out_ref,
    rs,
    rows,
    hs,
    head,
    cols,
    fact,
    upper,
    ready0,
    ready1,
    io,
    sc_send,
    sc_recv,
    sends,
    ra_recv,
    ha_recv,
    hz_send,
    hz_recv,
    z_recv,
    own_send,
    own_recv,
    zc_send,
    zc_recv,
    cc_send,
    cc_recv,
):
    p = lax.axis_index("prow")
    q = lax.axis_index("pcol")
    core = lax.rem(q, 2)
    chip = q // 2
    chip_y, chip_x = chip // SIDE, lax.rem(chip, SIDE)
    partner = q + 1 - 2 * core
    is_zero = core == 0
    is_one = core == 1
    is_root = p < PANELS
    scatters = (q == 0) | (q == 2)
    flows = chip > 0

    def remote(src, dst, send, recv, row, col):
        return pltpu.make_async_remote_copy(
            src_ref=src, dst_ref=dst, send_sem=send, recv_sem=recv, device_id=(row, col), device_id_type=MESH
        )

    def signal(sem, row, col):
        pl.semaphore_signal(sem, inc=1, device_id=(row, col), device_id_type=MESH)

    def count(flag):
        return flag.astype(jnp.int32)

    fetch = pltpu.make_async_copy(x_hbm, x_ref, io.at[0])
    fetch.start()

    barrier = pltpu.get_barrier_semaphore()

    def greet(steps, edge):
        for s in steps:
            child, parent = wrap(p + s), wrap(p - s)

            @pl.when(edge(s, p) & (p < child))
            def _():
                signal(barrier, child, q)

            @pl.when(edge(s, parent) & (parent > p))
            def _():
                signal(barrier, parent, q)

    def greetings(steps, edge, twice=()):
        total = 0
        for s in steps:
            child, parent = wrap(p + s), wrap(p - s)
            total = total + count(edge(s, parent) & (parent < p)) + (1 + (s in twice)) * count(edge(s, p) & (child < p))
        return total

    def answer(steps, edge, ready):
        for i, s in enumerate(steps):
            parent = wrap(p - s)

            @pl.when(edge(s, parent) & (parent < p))
            def _():
                signal(ready.at[i], parent, q)

    def await_ready(steps, edge, ready, s):
        @pl.when(edge(s, p) & (p < wrap(p + s)))
        def _():
            pl.semaphore_wait(ready.at[steps.index(s)], 1)

    @pl.when(is_zero)
    def _():
        @pl.when(flows)
        def _():
            greet(STEPS0, edge0)

        @pl.when(scatters)
        def _():
            @pl.loop(0, NC)
            def _(j):
                signal(barrier, p, 2 * j + 1)

        @pl.when(jnp.logical_not(scatters))
        def _():
            signal(barrier, p, partner)

        pl.semaphore_wait(barrier, greetings(STEPS0, edge0, (1, -1)) * count(flows) + 1 + (NC - 1) * count(scatters))

        @pl.when(flows)
        def _():
            answer(STEPS0, edge0, ready0)

    @pl.when(is_one)
    def _():
        greet(STEPS1, edge1)

        for s in (1, -1):
            parent = wrap(p - s)

            @pl.when(flows & edge0(s, parent) & (parent > p))
            def _():
                signal(barrier, parent, partner)

        for step in (1, -1):
            signal(barrier, p, 2 * (chip_y * SIDE + lax.rem(chip_x + step + SIDE, SIDE)) + 1)
            signal(barrier, p, 2 * (lax.rem(chip_y + step + SIDE, SIDE) * SIDE + chip_x) + 1)

        for t in range(PANELS):

            @pl.when((partner != t) & (q != t))
            def _():
                signal(barrier, p, t)

        @pl.when(q == 1)
        def _():
            @pl.loop(1, NC)
            def _(j):
                signal(barrier, p, 2 * j + 1)

        signal(barrier, p, partner)
        others = 4 + 4 - count((partner == 0) | (partner == 2)) + (NC - 2) * count(q == 1)
        pl.semaphore_wait(barrier, greetings(STEPS1, edge1) + others)
        answer(STEPS1, edge1, ready1)

    fetch.wait()

    def scatter(t, b):
        k = lax.rem(q, PANELS)
        return remote(x_ref.at[b, :, t], rs.at[k, b], sc_send.at[b], sc_recv.at[b, k], p, 2 * t + 1)

    def own(half):
        piece = cols.at[1, lax.rem(p, PANELS), half]
        return remote(x_ref.at[0, half], piece, own_send.at[half], own_recv.at[half], p, partner)

    @pl.when(is_one & is_root & flows)
    def _():
        own(0).start()
        own(1).start()

    @pl.when(q < PANELS)
    def _():
        for b in range(2):

            @pl.loop(0, NC)
            def _(t):
                @pl.when(2 * t + 1 != q)
                def _():
                    scatter(t, b).start()

    def col_piece(k, i):
        half, j = i // 4, lax.rem(i, 4)
        return cols.at[j // 2, k, half, pl.ds(lax.rem(j, 2) * (CR // S), CR // S)]

    def col_copy(k, half, i, step, slot=None):
        piece = col_piece(k, i)
        n = STEPS0.index(step)
        to = q + lax.rem(i, 4) // 2 if step in (1, -1) else q
        send = sends.at[(k * 2 + half) * 4 + n if slot is None else slot]
        return remote(piece, piece, send, z_recv.at[k * CHUNKS + i], wrap(p + step), to)

    def to_one(k, i):
        piece = col_piece(k, i)
        return remote(piece, piece, zc_send.at[k], zc_recv.at[k], p, partner)

    def live(i):
        return (chip > 1) | (lax.rem(i, 4) >= 2)

    def pass_on(k, i):
        away = wrap(p - k)
        for half in range(2):

            @pl.when(i // 4 == half)
            def _():
                for s in STEPS0:

                    @pl.when(among(away, ON[half][s]))
                    def _():
                        col_copy(k, half, i, s).start()

    def passed(k):
        away = wrap(p - k)
        for half in range(2):
            for n, s in enumerate(STEPS0):
                places = among(away, ON[half][s])
                for flag, piece in ((chip > 1, cols.at[:, k, half]), (chip == 1, cols.at[1, k, half])):

                    @pl.when(places & flag)
                    def _():
                        remote(piece, piece, sends.at[(k * 2 + half) * 4 + n], z_recv.at[0], p, partner).wait_send()

    def in_turn(k, i):
        away = wrap(p - k)
        return lax.rem(i + 4 * count(away > 8), CHUNKS)

    @pl.when(is_zero & flows)
    def _():
        mine = lax.rem(p, PANELS)

        def own_copy(n, step):
            i = lax.rem(n + (0 if step == 2 else 4), CHUNKS)
            return col_copy(mine, 0, i, step, 6 * 4 + (0 if step == 2 else WINDOW) + lax.rem(n, WINDOW))

        def start_own(n, step):
            @pl.when(is_root & (n < CHUNKS) & live(n))
            def _():
                @pl.when((n >= WINDOW) & live(n + CHUNKS - WINDOW))
                def _():
                    own_copy(n - WINDOW, step).wait_send()

                own_copy(n, step).start()

        @pl.when(is_root)
        def _():
            cols[0, mine] = x_ref[0]

        await_ready(STEPS0, edge0, ready0, 2)

        @pl.loop(0, CHUNKS + LAG)
        def _(n):
            for half, turn in ((0, 2), (1, LAG + 2)):

                @pl.when(is_root & (n == turn))
                def _():
                    own(half).wait_recv()

            start_own(n, 2)

            @pl.when(n == LAG)
            def _():
                for s in (-2, -1, 1):
                    await_ready(STEPS0, edge0, ready0, s)

            @pl.when(n >= LAG)
            def _():
                i = n - LAG
                start_own(i, -2)
                for k in reversed(range(PANELS)):
                    away = wrap(p - k)

                    @pl.when((lax.rem(away, 2) == 0) & (away != 0) & live(i))
                    def _():
                        t = in_turn(k, i)
                        col_copy(k, 0, t, 2).wait_recv()
                        pass_on(k, t)

                        @pl.when(lax.rem(t, 4) >= 2)
                        def _():
                            to_one(k, t).start()

        @pl.when(is_root)
        def _():
            @pl.loop(0, CHUNKS)
            def _(n):
                @pl.when(live(n) & ((n >= CHUNKS - WINDOW) | jnp.logical_not(live(n + WINDOW))))
                def _():
                    own_copy(n, 2).wait_send()
                    own_copy(n, -2).wait_send()

    def await_fills():
        @pl.when(flows)
        def _():
            for k in range(PANELS):

                @pl.when((lax.rem(wrap(p - k), 2) == 1) & (is_one | (chip > 1)))
                def _():
                    @pl.loop(0, CHUNKS // 2)
                    def _(i):
                        col_copy(k, 0, (i // 2) * 4 + core * 2 + lax.rem(i, 2), 2).wait_recv()

                @pl.when(is_one & (p != k) & (lax.rem(wrap(p - k), 2) == 0))
                def _():
                    remote(cols.at[1, k], cols.at[1, k], zc_send.at[k], zc_recv.at[k], p, partner).wait_recv()

    @pl.when((chip == 0) | ((chip == 1) & is_zero))
    def _():
        cols[core] = jnp.zeros_like(cols[core])

    def across(buffer, n, half, c):
        piece = buffer.at[half, c]
        return remote(piece, piece, cc_send.at[n], cc_recv.at[n], p, partner)

    def whole(buffer, n):
        return remote(buffer, buffer, cc_send.at[n], cc_recv.at[n], p, partner)

    class Ring:
        def __init__(self, buffer, recv, n, apart):
            self.buffer, self.recv, self.n, self.apart = buffer, recv, n, apart

        def line(self, stage, half, t, step):
            if stage == half:
                x = lax.rem(chip_x + step + SIDE, SIDE)
                return (chip_y if stage == 0 else t) * SIDE + x
            y = lax.rem(chip_y + step + SIDE, SIDE)
            return y * SIDE + (chip_x if stage == 0 else t)

        def neighbour(self, stage, half, step):
            if stage == half:
                return 2 * (chip_y * SIDE + lax.rem(chip_x + step + SIDE, SIDE)) + 1
            return 2 * (lax.rem(chip_y + step + SIDE, SIDE) * SIDE + chip_x) + 1

        def copy(self, stage, half, t, kind):
            step = 1 if kind in (0, 2) else -1
            piece = self.buffer.at[half, self.line(stage, half, t, 0 if kind < 2 else -step)]
            if kind >= 2:
                piece = piece.at[:, :, :, pl.ds((kind - 2) * (B // 2), B // 2)]
            return self.between(piece, stage, half, t, kind, self.neighbour(stage, half, step))

        def between(self, piece, stage, half, t, kind, to):
            i = kind * 4 + stage * 2 + half
            recv = self.recv.at[i]
            if self.apart and stage == 1 and kind < 2:
                recv = self.recv.at[16 + (kind * 2 + half) * SIDE + t]
            return remote(piece, piece, sends.at[self.n * 16 + i], recv, p, to)

        def all_of(self, stage, half, kind):
            piece = self.buffer.at[half, pl.ds(0, SIDE if stage else 1)]
            if kind >= 2:
                piece = piece.at[:, :, :, :, pl.ds(0, B // 2)]
            return self.between(piece, stage, half, 0, kind, partner)

        def each(self, stage, act):
            if stage == 0:
                for half in range(2):
                    act(half, 0)
                return

            @pl.loop(0, SIDE)
            def _(t):
                for half in range(2):
                    act(half, t)

        def push(self, stage, half, t, step):
            if stage == 1:
                across(self.buffer, self.n, half, self.line(stage, half, t, step)).start()

        def begin(self, stage):
            def act(half, t):
                self.copy(stage, half, t, 0).start()
                self.copy(stage, half, t, 1).start()
                self.push(stage, half, t, 0)

            self.each(stage, act)

        def middle(self, stage):
            apart = self.apart and stage == 1
            if not apart:
                for half in range(2):
                    for kind in range(2):
                        self.all_of(stage, half, kind).wait_recv()

            def act(half, t):
                for kind in range(2):
                    if apart:
                        self.copy(stage, half, t, kind).wait_recv()
                    self.copy(stage, half, t, 2 + kind).start()
                    self.push(stage, half, t, -1 if kind == 0 else 1)

            self.each(stage, act)

        def end(self, stage):
            for half in range(2):
                for kind in (2, 3):
                    self.all_of(stage, half, kind).wait_recv()
            self.each(stage, lambda half, t: self.push(stage, half, t, 2))

        def sent(self):
            for stage in range(2):
                for half in range(2):
                    for kind in range(4):
                        self.all_of(stage, half, kind).wait_send()

    near = lax.rem(p, 4)
    mine4 = lax.rem(near, PANELS)
    anchor = near < PANELS

    def along(step):
        n = STEPS1.index(step)
        return remote(hs.at[mine4], hs.at[mine4], hz_send.at[n], hz_recv.at[mine4], wrap(p + step), q)

    row_ring = Ring(rows, ra_recv, 0, False)
    head_ring = Ring(head, ha_recv, 1, True)

    @pl.when(is_one)
    def _():
        @pl.when(q == 1)
        def _():
            rs[1] = x_ref[:, :, 0]

        def scattered(b):
            for k in range(PANELS):

                @pl.when(q != k)
                def _():
                    remote(x_ref.at[b, :, 0], rs.at[k, b], sc_send.at[b], sc_recv.at[b, k], p, partner).wait_recv()

        @pl.when(is_root)
        def _():
            scattered(0)
            hs[mine4] = rs[:, 0]

        @pl.when(anchor & jnp.logical_not(is_root))
        def _():
            along(4).wait_recv()

        for s in STEPS1:
            await_ready(STEPS1, edge1, ready1, s)

            @pl.when(edge1(s, p))
            def _():
                along(s).start()

        @pl.when(jnp.logical_not(is_root))
        def _():
            scattered(0)

        scattered(1)
        for half in range(2):
            rows[half, chip] = rs[:, :, half]
        row_ring.begin(0)

        for k in range(PANELS):

            @pl.when(near != k)
            def _():
                remote(hs.at[k], hs.at[k], hz_send.at[0], hz_recv.at[k], p, partner).wait_recv()

        for half in range(2):
            head[half, chip] = hs[:, :, half]
        head_ring.begin(0)
        head_ring.middle(0)
        head_ring.end(0)
        head_ring.begin(1)
        row_ring.middle(0)

        @pl.when(is_root & flows)
        def _():
            cols[1, lax.rem(p, PANELS)] = x_ref[0]

        head_ring.middle(1)
        row_ring.end(0)
        row_ring.begin(1)
        head_ring.end(1)

    @pl.when(is_zero)
    def _():
        whole(head, 1).wait_recv()

    def block(i, j):
        return head[:, :, i, j].reshape(B, B)

    a = {(i, j): block(i, j) for i in range(PANELS) for j in range(PANELS)}
    halves = {}
    for k in range(PANELS):
        inverse = invert(a[k, k])
        fact[k, k] = inverse
        halves[k, k] = split(inverse)
        below = range(k + 1, PANELS)
        if below:
            for i, factor in zip(below, products([split(a[i, k]) for i in below], halves[k, k])):
                fact[i, k] = factor
                halves[i, k] = split(factor)
        for j in below:
            fact[k, j] = a[k, j]
            halves[k, j] = split(a[k, j])
            for i, update in zip(below, products([halves[i, k] for i in below], halves[k, j])):
                a[i, j] = a[i, j] - update
        if k == 1:

            @pl.when(is_one)
            def _():
                row_ring.middle(1)

    await_fills()
    is_panel = q < PANELS
    eye = (
        lax.broadcasted_iota(jnp.int32, (B, B), 0) == lax.broadcasted_iota(jnp.int32, (B, B), 1)
    ).astype(jnp.float32)
    value = [cols[core, i].reshape(B, B) for i in range(PANELS)]
    for i in range(PANELS):
        upper[i] = value[i]
        later = range(i + 1, PANELS)
        if later:
            for m, update in zip(later, products([halves[m, i] for m in later], split(value[i]))):
                value[m] = value[m] - update

    right = [None] * PANELS
    value = [jnp.where(is_panel, jnp.where(q == i, eye, 0.0), upper[i]) for i in range(PANELS)]
    for i in reversed(range(PANELS)):
        right[i] = split(product(halves[i, i], split(value[i])))
        if i:
            for m, update in zip(range(i), products([halves[m, i] for m in range(i)], right[i])):
                value[m] = value[m] - update

    @pl.when(is_one)
    def _():
        row_ring.end(1)

    @pl.when(is_zero)
    def _():
        whole(rows, 0).wait_recv()

    keep = jnp.where(is_panel, 0.0, 1.0)
    sign = jnp.where(is_panel, 1.0, -1.0)
    total = [None, None]
    for k in range(PANELS):
        panel = [split(rows[:, :, k, b].reshape(B, B)) for b in range(2)]
        for b, term in enumerate(products(panel, right[k])):
            total[b] = term if k == 0 else total[b] + term
    def store(b):
        return pltpu.make_async_copy(out_ref.at[b], out_hbm.at[b], io.at[1 + b])

    out_ref[1] = keep * x_ref[1].reshape(B, B) + sign * total[1]
    store(1).start()

    @pl.when(jnp.logical_not(is_root))
    def _():
        out_ref[0] = keep * x_ref[0].reshape(B, B) + sign * total[0]

    @pl.when(is_root & is_panel)
    def _():
        out_ref[0] = fact[lax.rem(p, PANELS), lax.rem(q, PANELS)]

    @pl.when(is_root & (q >= PANELS))
    def _():
        out_ref[0] = upper[lax.rem(p, PANELS)]

    store(0).start()

    for b in range(2):
        for pieces, flag in ((NC - 1, q == 1), (NC, scatters)):

            @pl.when(flag)
            def _():
                piece = x_ref.at[b, :, pl.ds(0, pieces)]
                remote(piece, piece, sc_send.at[b], sc_recv.at[b, 0], p, partner).wait_send()

    @pl.when(is_zero & flows)
    def _():
        for k in range(PANELS):

            @pl.when(p != k)
            def _():
                passed(k)

            @pl.when((p != k) & (lax.rem(wrap(p - k), 2) == 0))
            def _():
                remote(cols.at[1, k], cols.at[1, k], zc_send.at[k], zc_recv.at[k], p, partner).wait_send()

    @pl.when(is_one)
    def _():
        @pl.when(is_root & flows)
        def _():
            own(0).wait_send()
            own(1).wait_send()

        for s in STEPS1:

            @pl.when(edge1(s, p))
            def _():
                along(s).wait_send()

        row_ring.sent()
        head_ring.sent()
        whole(rows, 0).wait_send()
        whole(head, 1).wait_send()

    store(0).wait()
    store(1).wait()


def body(matrix):
    shape = matrix.shape
    f32 = jnp.float32
    dma = pltpu.SemaphoreType.DMA
    out = pl.pallas_call(
        kernel,
        out_shape=jax.ShapeDtypeStruct((2, B, B), f32),
        in_specs=[pl.BlockSpec(memory_space=pl.ANY)],
        out_specs=pl.BlockSpec(memory_space=pl.ANY),
        scratch_shapes=[
            pltpu.VMEM((2, 2, NC, S, B), f32),
            pltpu.VMEM((2, B, B), f32),
            pltpu.VMEM((PANELS, 2, 2, S, B), f32),
            pltpu.VMEM((2, NC, PANELS, 2, S, B), f32),
            pltpu.VMEM((PANELS, PANELS, 2, S, B), f32),
            pltpu.VMEM((2, NC, PANELS, PANELS, S, B), f32),
            pltpu.VMEM((2, PANELS, 2, NC, S, B), f32),
            pltpu.VMEM((PANELS, PANELS, B, B), f32),
            pltpu.VMEM((PANELS, B, B), f32),
            pltpu.SemaphoreType.REGULAR((len(STEPS0),)),
            pltpu.SemaphoreType.REGULAR((len(STEPS1),)),
            dma((3,)),
            dma((2,)),
            dma((2, PANELS)),
            dma((32,)),
            dma((16,)),
            dma((32,)),
            dma((len(STEPS1),)),
            dma((PANELS,)),
            dma((PANELS * CHUNKS,)),
            dma((2,)),
            dma((2,)),
            dma((PANELS,)),
            dma((PANELS,)),
            dma((2,)),
            dma((2,)),
        ],
        compiler_params=pltpu.CompilerParams(
            collective_id=0, has_side_effects=True, vmem_limit_bytes=48 * 1024 * 1024
        ),
    )(matrix.reshape(2, 2, NC, S, B))
    return out.reshape(shape)


def solution(mesh):
    spec = P(None, "prow", None, "pcol", None)
    return jax.shard_map(body, mesh=mesh, in_specs=(spec,), out_specs=spec, check_vma=False)
```

```python
import functools

import jax
import jax.numpy as jnp
from jax import lax
from jax.experimental import pallas as pl
from jax.experimental.pallas import tpu as pltpu
from jax.sharding import PartitionSpec as P

B = 256
PANELS = 3
NP = 16
NQ = 32
NC = NQ // 2
S = B // NC // 2
SIDE = 4
CHUNKS = 8
CR = 2 * B // CHUNKS
WINDOW = 2
LAG = 3
MESH = pl.DeviceIdType.MESH
STEPS0 = (2, 1, -1, -2)
STEPS1 = (4, 1, -1, -2, -4)


def split(value):
    high = value.astype(jnp.bfloat16)
    return high, (value - high.astype(jnp.float32)).astype(jnp.bfloat16)


def products(lefts, right):
    dot = functools.partial(jnp.dot, preferred_element_type=jnp.float32)
    return [dot(left[0], right[0]) + (dot(left[0], right[1]) + dot(left[1], right[0])) for left in lefts]


def product(left, right):
    return products([left], right)[0]


def invert(block):
    row = lax.broadcasted_iota(jnp.int32, (B, B), 0)
    col = lax.broadcasted_iota(jnp.int32, (B, B), 1)
    eye = row == col
    diagonal = jnp.where(eye, block, 0.0)
    down = 1.0 / jnp.sum(diagonal, axis=1, keepdims=True)
    across = 1.0 / jnp.sum(diagonal, axis=0, keepdims=True)
    first = jnp.where(eye, 2.0 * down, 0.0) - down * block * across
    parts = split(first)
    inner = product(split(block), parts)
    return 2.0 * first - product(parts, split(inner))


def wrap(p):
    return lax.rem(p + 2 * NP, NP)


def among(value, choices):
    found = value == choices[0]
    for c in choices[1:]:
        found = found | (value == c)
    return found


ON = (
    {2: (0, 2, 4, 6, 8), -2: (0, 14), -1: (2, 4, 6, 8, 10), 1: (10, 12, 14)},
    {2: (0, 2, 4), -2: (0, 14, 12, 10), -1: (2, 4, 6), 1: (6, 8, 10, 12, 14)},
)


def edge0(step, p):
    places = sorted(set(ON[0][step]) | set(ON[1][step]))
    found = among(wrap(p), places)
    for k in range(1, PANELS):
        found = found | among(wrap(p - k), places)
    return found


def edge1(step, p):
    near = lax.rem(p, 4)
    if step == 4:
        return (near < PANELS) & (p < 8)
    if step == -4:
        return p < PANELS
    return near < PANELS


def kernel(
    x_hbm,
    out_hbm,
    x_ref,
    out_ref,
    rs,
    rows,
    hs,
    head,
    cols,
    fact,
    upper,
    ready0,
    ready1,
    io,
    sc_send,
    sc_recv,
    sends,
    ra_recv,
    ha_recv,
    hz_send,
    hz_recv,
    z_recv,
    own_send,
    own_recv,
    zc_send,
    zc_recv,
    cc_send,
    cc_recv,
):
    p = lax.axis_index("prow")
    q = lax.axis_index("pcol")
    core = lax.rem(q, 2)
    chip = q // 2
    chip_y, chip_x = chip // SIDE, lax.rem(chip, SIDE)
    partner = q + 1 - 2 * core
    is_zero = core == 0
    is_one = core == 1
    is_root = p < PANELS
    scatters = (q == 0) | (q == 2)
    flows = chip > 0

    def remote(src, dst, send, recv, row, col):
        return pltpu.make_async_remote_copy(
            src_ref=src, dst_ref=dst, send_sem=send, recv_sem=recv, device_id=(row, col), device_id_type=MESH
        )

    def signal(sem, row, col):
        pl.semaphore_signal(sem, inc=1, device_id=(row, col), device_id_type=MESH)

    def count(flag):
        return flag.astype(jnp.int32)

    fetch = pltpu.make_async_copy(x_hbm, x_ref, io.at[0])
    fetch.start()

    barrier = pltpu.get_barrier_semaphore()

    def greet(steps, edge):
        for s in steps:
            child, parent = wrap(p + s), wrap(p - s)

            @pl.when(edge(s, p) & (p < child))
            def _():
                signal(barrier, child, q)

            @pl.when(edge(s, parent) & (parent > p))
            def _():
                signal(barrier, parent, q)

    def greetings(steps, edge, twice=()):
        total = 0
        for s in steps:
            child, parent = wrap(p + s), wrap(p - s)
            total = total + count(edge(s, parent) & (parent < p)) + (1 + (s in twice)) * count(edge(s, p) & (child < p))
        return total

    def answer(steps, edge, ready):
        for i, s in enumerate(steps):
            parent = wrap(p - s)

            @pl.when(edge(s, parent) & (parent < p))
            def _():
                signal(ready.at[i], parent, q)

    def await_ready(steps, edge, ready, s):
        @pl.when(edge(s, p) & (p < wrap(p + s)))
        def _():
            pl.semaphore_wait(ready.at[steps.index(s)], 1)

    @pl.when(is_zero)
    def _():
        @pl.when(flows)
        def _():
            greet(STEPS0, edge0)

        @pl.when(scatters)
        def _():
            @pl.loop(0, NC)
            def _(j):
                signal(barrier, p, 2 * j + 1)

        @pl.when(jnp.logical_not(scatters))
        def _():
            signal(barrier, p, partner)

        pl.semaphore_wait(barrier, greetings(STEPS0, edge0, (1, -1)) * count(flows) + 1 + (NC - 1) * count(scatters))

        @pl.when(flows)
        def _():
            answer(STEPS0, edge0, ready0)

    @pl.when(is_one)
    def _():
        greet(STEPS1, edge1)

        for s in (1, -1):
            parent = wrap(p - s)

            @pl.when(flows & edge0(s, parent) & (parent > p))
            def _():
                signal(barrier, parent, partner)

        for step in (1, -1):
            signal(barrier, p, 2 * (chip_y * SIDE + lax.rem(chip_x + step + SIDE, SIDE)) + 1)
            signal(barrier, p, 2 * (lax.rem(chip_y + step + SIDE, SIDE) * SIDE + chip_x) + 1)

        for t in range(PANELS):

            @pl.when((partner != t) & (q != t))
            def _():
                signal(barrier, p, t)

        @pl.when(q == 1)
        def _():
            @pl.loop(1, NC)
            def _(j):
                signal(barrier, p, 2 * j + 1)

        signal(barrier, p, partner)
        others = 4 + 4 - count((partner == 0) | (partner == 2)) + (NC - 2) * count(q == 1)
        pl.semaphore_wait(barrier, greetings(STEPS1, edge1) + others)
        answer(STEPS1, edge1, ready1)

    fetch.wait()

    def scatter(t, b):
        k = lax.rem(q, PANELS)
        return remote(x_ref.at[b, :, t], rs.at[k, b], sc_send.at[b], sc_recv.at[b, k], p, 2 * t + 1)

    def own(half):
        piece = cols.at[1, lax.rem(p, PANELS), half]
        return remote(x_ref.at[0, half], piece, own_send.at[half], own_recv.at[half], p, partner)

    @pl.when(is_one & is_root & flows)
    def _():
        own(0).start()
        own(1).start()

    @pl.when(q < PANELS)
    def _():
        for b in range(2):

            @pl.loop(0, NC)
            def _(t):
                @pl.when(2 * t + 1 != q)
                def _():
                    scatter(t, b).start()

    def col_piece(k, i):
        half, j = i // 4, lax.rem(i, 4)
        return cols.at[j // 2, k, half, pl.ds(lax.rem(j, 2) * (CR // S), CR // S)]

    def col_copy(k, half, i, step, slot=None):
        piece = col_piece(k, i)
        n = STEPS0.index(step)
        to = q + lax.rem(i, 4) // 2 if step in (1, -1) else q
        send = sends.at[(k * 2 + half) * 4 + n if slot is None else slot]
        return remote(piece, piece, send, z_recv.at[k * CHUNKS + i], wrap(p + step), to)

    def to_one(k, i):
        piece = col_piece(k, i)
        return remote(piece, piece, zc_send.at[k], zc_recv.at[k], p, partner)

    def live(i):
        return (chip > 1) | (lax.rem(i, 4) >= 2)

    def pass_on(k, i):
        away = wrap(p - k)
        for half in range(2):

            @pl.when(i // 4 == half)
            def _():
                for s in STEPS0:

                    @pl.when(among(away, ON[half][s]))
                    def _():
                        col_copy(k, half, i, s).start()

    def passed(k):
        away = wrap(p - k)
        for half in range(2):
            for n, s in enumerate(STEPS0):
                places = among(away, ON[half][s])
                for flag, piece in ((chip > 1, cols.at[:, k, half]), (chip == 1, cols.at[1, k, half])):

                    @pl.when(places & flag)
                    def _():
                        remote(piece, piece, sends.at[(k * 2 + half) * 4 + n], z_recv.at[0], p, partner).wait_send()

    def in_turn(k, i):
        away = wrap(p - k)
        return lax.rem(i + 4 * count(away > 8), CHUNKS)

    @pl.when(is_zero & flows)
    def _():
        mine = lax.rem(p, PANELS)

        def own_copy(n, step):
            i = lax.rem(n + (0 if step == 2 else 4), CHUNKS)
            return col_copy(mine, 0, i, step, 6 * 4 + (0 if step == 2 else WINDOW) + lax.rem(n, WINDOW))

        def start_own(n, step):
            @pl.when(is_root & (n < CHUNKS) & live(n))
            def _():
                @pl.when((n >= WINDOW) & live(n + CHUNKS - WINDOW))
                def _():
                    own_copy(n - WINDOW, step).wait_send()

                own_copy(n, step).start()

        @pl.when(is_root)
        def _():
            cols[0, mine] = x_ref[0]

        await_ready(STEPS0, edge0, ready0, 2)

        @pl.loop(0, CHUNKS + LAG)
        def _(n):
            for half, turn in ((0, 2), (1, LAG + 2)):

                @pl.when(is_root & (n == turn))
                def _():
                    own(half).wait_recv()

            start_own(n, 2)

            @pl.when(n == LAG)
            def _():
                for s in (-2, -1, 1):
                    await_ready(STEPS0, edge0, ready0, s)

            @pl.when(n >= LAG)
            def _():
                i = n - LAG
                start_own(i, -2)
                for k in reversed(range(PANELS)):
                    away = wrap(p - k)

                    @pl.when((lax.rem(away, 2) == 0) & (away != 0) & live(i))
                    def _():
                        t = in_turn(k, i)
                        col_copy(k, 0, t, 2).wait_recv()
                        pass_on(k, t)

                        @pl.when(lax.rem(t, 4) >= 2)
                        def _():
                            to_one(k, t).start()

        @pl.when(is_root)
        def _():
            @pl.loop(0, CHUNKS)
            def _(n):
                @pl.when(live(n) & ((n >= CHUNKS - WINDOW) | jnp.logical_not(live(n + WINDOW))))
                def _():
                    own_copy(n, 2).wait_send()
                    own_copy(n, -2).wait_send()

    def await_fills():
        @pl.when(flows)
        def _():
            for k in range(PANELS):

                @pl.when((lax.rem(wrap(p - k), 2) == 1) & (is_one | (chip > 1)))
                def _():
                    @pl.loop(0, CHUNKS // 2)
                    def _(i):
                        col_copy(k, 0, (i // 2) * 4 + core * 2 + lax.rem(i, 2), 2).wait_recv()

                @pl.when(is_one & (p != k) & (lax.rem(wrap(p - k), 2) == 0))
                def _():
                    remote(cols.at[1, k], cols.at[1, k], zc_send.at[k], zc_recv.at[k], p, partner).wait_recv()

    @pl.when((chip == 0) | ((chip == 1) & is_zero))
    def _():
        cols[core] = jnp.zeros_like(cols[core])

    def across(buffer, n, half, c):
        piece = buffer.at[half, c]
        return remote(piece, piece, cc_send.at[n], cc_recv.at[n], p, partner)

    def whole(buffer, n):
        return remote(buffer, buffer, cc_send.at[n], cc_recv.at[n], p, partner)

    class Ring:
        def __init__(self, buffer, recv, n, apart):
            self.buffer, self.recv, self.n, self.apart = buffer, recv, n, apart

        def line(self, stage, half, t, step):
            if stage == half:
                x = lax.rem(chip_x + step + SIDE, SIDE)
                return (chip_y if stage == 0 else t) * SIDE + x
            y = lax.rem(chip_y + step + SIDE, SIDE)
            return y * SIDE + (chip_x if stage == 0 else t)

        def neighbour(self, stage, half, step):
            if stage == half:
                return 2 * (chip_y * SIDE + lax.rem(chip_x + step + SIDE, SIDE)) + 1
            return 2 * (lax.rem(chip_y + step + SIDE, SIDE) * SIDE + chip_x) + 1

        def copy(self, stage, half, t, kind):
            step = 1 if kind in (0, 2) else -1
            piece = self.buffer.at[half, self.line(stage, half, t, 0 if kind < 2 else -step)]
            if kind >= 2:
                piece = piece.at[:, :, :, pl.ds((kind - 2) * (B // 2), B // 2)]
            return self.between(piece, stage, half, t, kind, self.neighbour(stage, half, step))

        def between(self, piece, stage, half, t, kind, to):
            i = kind * 4 + stage * 2 + half
            recv = self.recv.at[i]
            if self.apart and stage == 1 and kind < 2:
                recv = self.recv.at[16 + (kind * 2 + half) * SIDE + t]
            return remote(piece, piece, sends.at[self.n * 16 + i], recv, p, to)

        def all_of(self, stage, half, kind):
            piece = self.buffer.at[half, pl.ds(0, SIDE if stage else 1)]
            if kind >= 2:
                piece = piece.at[:, :, :, :, pl.ds(0, B // 2)]
            return self.between(piece, stage, half, 0, kind, partner)

        def each(self, stage, act, offsets=(0, 1, 3, 2)):
            for offset in offsets if stage else (0,):
                for half in range(2):
                    act(half, lax.rem((chip_y if half else chip_x) + offset, SIDE) if stage else 0)

        def push(self, stage, half, t, step):
            if stage == 1:
                across(self.buffer, self.n, half, self.line(stage, half, t, step)).start()

        def begin(self, stage, offsets=(0, 1, 3, 2)):
            def act(half, t):
                self.copy(stage, half, t, 0).start()
                self.copy(stage, half, t, 1).start()
                self.push(stage, half, t, 0)

            self.each(stage, act, offsets)

        def middle(self, stage):
            apart = self.apart and stage == 1
            if not apart:
                for half in range(2):
                    for kind in range(2):
                        self.all_of(stage, half, kind).wait_recv()

            def act(half, t):
                for kind in range(2):
                    if apart:
                        self.copy(stage, half, t, kind).wait_recv()
                    self.copy(stage, half, t, 2 + kind).start()
                    self.push(stage, half, t, -1 if kind == 0 else 1)

            self.each(stage, act)

        def end(self, stage):
            for half in range(2):
                for kind in (2, 3):
                    self.all_of(stage, half, kind).wait_recv()
            self.each(stage, lambda half, t: self.push(stage, half, t, 2))

        def sent(self):
            for stage in range(2):
                for half in range(2):
                    for kind in range(4):
                        self.all_of(stage, half, kind).wait_send()

    near = lax.rem(p, 4)
    mine4 = lax.rem(near, PANELS)
    anchor = near < PANELS

    def along(step):
        n = STEPS1.index(step)
        return remote(hs.at[mine4], hs.at[mine4], hz_send.at[n], hz_recv.at[mine4], wrap(p + step), q)

    row_ring = Ring(rows, ra_recv, 0, False)
    head_ring = Ring(head, ha_recv, 1, True)

    @pl.when(is_one)
    def _():
        @pl.when(q == 1)
        def _():
            rs[1] = x_ref[:, :, 0]

        def scattered(b):
            for k in range(PANELS):

                @pl.when(q != k)
                def _():
                    remote(x_ref.at[b, :, 0], rs.at[k, b], sc_send.at[b], sc_recv.at[b, k], p, partner).wait_recv()

        @pl.when(is_root)
        def _():
            scattered(0)
            hs[mine4] = rs[:, 0]

        @pl.when(anchor & jnp.logical_not(is_root))
        def _():
            along(4).wait_recv()

        for s in STEPS1:
            await_ready(STEPS1, edge1, ready1, s)

            @pl.when(edge1(s, p))
            def _():
                along(s).start()

        @pl.when(jnp.logical_not(is_root))
        def _():
            scattered(0)

        scattered(1)
        for half in range(2):
            rows[half, chip] = rs[:, :, half]
        row_ring.begin(0)

        for k in range(PANELS):

            @pl.when(near != k)
            def _():
                remote(hs.at[k], hs.at[k], hz_send.at[0], hz_recv.at[k], p, partner).wait_recv()

        for half in range(2):
            head[half, chip] = hs[:, :, half]
        head_ring.begin(0)
        head_ring.begin(1, (0,))
        head_ring.middle(0)
        head_ring.begin(1, (1, 3))
        head_ring.end(0)
        head_ring.begin(1, (2,))
        row_ring.middle(0)

        @pl.when(is_root & flows)
        def _():
            cols[1, lax.rem(p, PANELS)] = x_ref[0]

        head_ring.middle(1)
        row_ring.end(0)
        row_ring.begin(1)
        head_ring.end(1)

    @pl.when(is_zero)
    def _():
        whole(head, 1).wait_recv()

    def block(i, j):
        return head[:, :, i, j].reshape(B, B)

    a = {(i, j): block(i, j) for i in range(PANELS) for j in range(PANELS)}
    halves = {}
    for k in range(PANELS):
        inverse = invert(a[k, k])
        fact[k, k] = inverse
        halves[k, k] = split(inverse)
        below = range(k + 1, PANELS)
        if below:
            for i, factor in zip(below, products([split(a[i, k]) for i in below], halves[k, k])):
                fact[i, k] = factor
                halves[i, k] = split(factor)
        for j in below:
            fact[k, j] = a[k, j]
            halves[k, j] = split(a[k, j])
            for i, update in zip(below, products([halves[i, k] for i in below], halves[k, j])):
                a[i, j] = a[i, j] - update
        if k == 1:

            @pl.when(is_one)
            def _():
                row_ring.middle(1)

    await_fills()
    is_panel = q < PANELS
    eye = (
        lax.broadcasted_iota(jnp.int32, (B, B), 0) == lax.broadcasted_iota(jnp.int32, (B, B), 1)
    ).astype(jnp.float32)
    value = [cols[core, i].reshape(B, B) for i in range(PANELS)]
    for i in range(PANELS):
        upper[i] = value[i]
        later = range(i + 1, PANELS)
        if later:
            for m, update in zip(later, products([halves[m, i] for m in later], split(value[i]))):
                value[m] = value[m] - update

    right = [None] * PANELS
    value = [jnp.where(is_panel, jnp.where(q == i, eye, 0.0), upper[i]) for i in range(PANELS)]
    for i in reversed(range(PANELS)):
        right[i] = split(product(halves[i, i], split(value[i])))
        if i:
            for m, update in zip(range(i), products([halves[m, i] for m in range(i)], right[i])):
                value[m] = value[m] - update

    @pl.when(is_one)
    def _():
        row_ring.end(1)

    @pl.when(is_zero)
    def _():
        whole(rows, 0).wait_recv()

    keep = jnp.where(is_panel, 0.0, 1.0)
    sign = jnp.where(is_panel, 1.0, -1.0)
    total = [None, None]
    for k in range(PANELS):
        panel = [split(rows[:, :, k, b].reshape(B, B)) for b in range(2)]
        for b, term in enumerate(products(panel, right[k])):
            total[b] = term if k == 0 else total[b] + term
    def store(b):
        return pltpu.make_async_copy(out_ref.at[b], out_hbm.at[b], io.at[1 + b])

    out_ref[1] = keep * x_ref[1].reshape(B, B) + sign * total[1]
    store(1).start()

    @pl.when(jnp.logical_not(is_root))
    def _():
        out_ref[0] = keep * x_ref[0].reshape(B, B) + sign * total[0]

    @pl.when(is_root & is_panel)
    def _():
        out_ref[0] = fact[lax.rem(p, PANELS), lax.rem(q, PANELS)]

    @pl.when(is_root & (q >= PANELS))
    def _():
        out_ref[0] = upper[lax.rem(p, PANELS)]

    store(0).start()

    for b in range(2):
        for pieces, flag in ((NC - 1, q == 1), (NC, scatters)):

            @pl.when(flag)
            def _():
                piece = x_ref.at[b, :, pl.ds(0, pieces)]
                remote(piece, piece, sc_send.at[b], sc_recv.at[b, 0], p, partner).wait_send()

    @pl.when(is_zero & flows)
    def _():
        for k in range(PANELS):

            @pl.when(p != k)
            def _():
                passed(k)

            @pl.when((p != k) & (lax.rem(wrap(p - k), 2) == 0))
            def _():
                remote(cols.at[1, k], cols.at[1, k], zc_send.at[k], zc_recv.at[k], p, partner).wait_send()

    @pl.when(is_one)
    def _():
        @pl.when(is_root & flows)
        def _():
            own(0).wait_send()
            own(1).wait_send()

        for s in STEPS1:

            @pl.when(edge1(s, p))
            def _():
                along(s).wait_send()

        row_ring.sent()
        head_ring.sent()
        whole(rows, 0).wait_send()
        whole(head, 1).wait_send()

    store(0).wait()
    store(1).wait()


def body(matrix):
    shape = matrix.shape
    f32 = jnp.float32
    dma = pltpu.SemaphoreType.DMA
    out = pl.pallas_call(
        kernel,
        out_shape=jax.ShapeDtypeStruct((2, B, B), f32),
        in_specs=[pl.BlockSpec(memory_space=pl.ANY)],
        out_specs=pl.BlockSpec(memory_space=pl.ANY),
        scratch_shapes=[
            pltpu.VMEM((2, 2, NC, S, B), f32),
            pltpu.VMEM((2, B, B), f32),
            pltpu.VMEM((PANELS, 2, 2, S, B), f32),
            pltpu.VMEM((2, NC, PANELS, 2, S, B), f32),
            pltpu.VMEM((PANELS, PANELS, 2, S, B), f32),
            pltpu.VMEM((2, NC, PANELS, PANELS, S, B), f32),
            pltpu.VMEM((2, PANELS, 2, NC, S, B), f32),
            pltpu.VMEM((PANELS, PANELS, B, B), f32),
            pltpu.VMEM((PANELS, B, B), f32),
            pltpu.SemaphoreType.REGULAR((len(STEPS0),)),
            pltpu.SemaphoreType.REGULAR((len(STEPS1),)),
            dma((3,)),
            dma((2,)),
            dma((2, PANELS)),
            dma((32,)),
            dma((16,)),
            dma((32,)),
            dma((len(STEPS1),)),
            dma((PANELS,)),
            dma((PANELS * CHUNKS,)),
            dma((2,)),
            dma((2,)),
            dma((PANELS,)),
            dma((PANELS,)),
            dma((2,)),
            dma((2,)),
        ],
        compiler_params=pltpu.CompilerParams(
            collective_id=0, has_side_effects=True, vmem_limit_bytes=48 * 1024 * 1024
        ),
    )(matrix.reshape(2, 2, NC, S, B))
    return out.reshape(shape)


def solution(mesh):
    spec = P(None, "prow", None, "pcol", None)
    return jax.shard_map(body, mesh=mesh, in_specs=(spec,), out_specs=spec, check_vma=False)
```

```python
import functools

import jax
import jax.numpy as jnp
from jax import lax
from jax.experimental import pallas as pl
from jax.experimental.pallas import tpu as pltpu
from jax.sharding import PartitionSpec as P

B = 256
PANELS = 3
NP = 16
NQ = 32
NC = NQ // 2
S = B // NC // 2
SIDE = 4
CHUNKS = 8
CR = 2 * B // CHUNKS
WINDOW = 2
LAG = 4
MESH = pl.DeviceIdType.MESH
STEPS0 = (2, 1, -1, -2)
STEPS1 = (4, 1, -1, -2, -4)


def split(value):
    high = value.astype(jnp.bfloat16)
    return high, (value - high.astype(jnp.float32)).astype(jnp.bfloat16)


def products(lefts, right):
    dot = functools.partial(jnp.dot, preferred_element_type=jnp.float32)
    return [dot(left[0], right[0]) + (dot(left[0], right[1]) + dot(left[1], right[0])) for left in lefts]


def product(left, right):
    return products([left], right)[0]


def invert(block):
    row = lax.broadcasted_iota(jnp.int32, (B, B), 0)
    col = lax.broadcasted_iota(jnp.int32, (B, B), 1)
    eye = row == col
    diagonal = jnp.where(eye, block, 0.0)
    down = 1.0 / jnp.sum(diagonal, axis=1, keepdims=True)
    across = 1.0 / jnp.sum(diagonal, axis=0, keepdims=True)
    first = jnp.where(eye, 2.0 * down, 0.0) - down * block * across
    parts = split(first)
    inner = product(split(block), parts)
    return 2.0 * first - product(parts, split(inner))


def wrap(p):
    return lax.rem(p + 2 * NP, NP)


def among(value, choices):
    found = value == choices[0]
    for c in choices[1:]:
        found = found | (value == c)
    return found


ON = (
    {2: (0, 2, 4, 6, 8), -2: (0, 14), -1: (2, 4, 6, 8, 10), 1: (10, 12, 14)},
    {2: (0, 2, 4), -2: (0, 14, 12, 10), -1: (2, 4, 6), 1: (6, 8, 10, 12, 14)},
)


def edge0(step, p):
    places = sorted(set(ON[0][step]) | set(ON[1][step]))
    found = among(wrap(p), places)
    for k in range(1, PANELS):
        found = found | among(wrap(p - k), places)
    return found


def edge1(step, p):
    near = lax.rem(p, 4)
    if step == 4:
        return (near < PANELS) & (p < 8)
    if step == -4:
        return p < PANELS
    return near < PANELS


def kernel(
    x_hbm,
    out_hbm,
    x_ref,
    out_ref,
    rs,
    rows,
    hs,
    head,
    cols,
    fact,
    upper,
    ready0,
    ready1,
    io,
    sc_send,
    sc_recv,
    sends,
    ra_recv,
    ha_recv,
    hz_send,
    hz_recv,
    z_recv,
    own_send,
    own_recv,
    zc_send,
    zc_recv,
    cc_send,
    cc_recv,
):
    p = lax.axis_index("prow")
    q = lax.axis_index("pcol")
    core = lax.rem(q, 2)
    chip = q // 2
    chip_y, chip_x = chip // SIDE, lax.rem(chip, SIDE)
    partner = q + 1 - 2 * core
    is_zero = core == 0
    is_one = core == 1
    is_root = p < PANELS
    scatters = (q == 0) | (q == 2)
    flows = chip > 0

    def remote(src, dst, send, recv, row, col):
        return pltpu.make_async_remote_copy(
            src_ref=src, dst_ref=dst, send_sem=send, recv_sem=recv, device_id=(row, col), device_id_type=MESH
        )

    def signal(sem, row, col):
        pl.semaphore_signal(sem, inc=1, device_id=(row, col), device_id_type=MESH)

    def count(flag):
        return flag.astype(jnp.int32)

    fetch = pltpu.make_async_copy(x_hbm, x_ref, io.at[0])
    fetch.start()

    barrier = pltpu.get_barrier_semaphore()

    def greet(steps, edge):
        for s in steps:
            child, parent = wrap(p + s), wrap(p - s)

            @pl.when(edge(s, p) & (p < child))
            def _():
                signal(barrier, child, q)

            @pl.when(edge(s, parent) & (parent > p))
            def _():
                signal(barrier, parent, q)

    def greetings(steps, edge, twice=()):
        total = 0
        for s in steps:
            child, parent = wrap(p + s), wrap(p - s)
            total = total + count(edge(s, parent) & (parent < p)) + (1 + (s in twice)) * count(edge(s, p) & (child < p))
        return total

    def answer(steps, edge, ready):
        for i, s in enumerate(steps):
            parent = wrap(p - s)

            @pl.when(edge(s, parent) & (parent < p))
            def _():
                signal(ready.at[i], parent, q)

    def await_ready(steps, edge, ready, s):
        @pl.when(edge(s, p) & (p < wrap(p + s)))
        def _():
            pl.semaphore_wait(ready.at[steps.index(s)], 1)

    @pl.when(is_zero)
    def _():
        @pl.when(flows)
        def _():
            greet(STEPS0, edge0)

        @pl.when(scatters)
        def _():
            @pl.loop(0, NC)
            def _(j):
                signal(barrier, p, 2 * j + 1)

        @pl.when(jnp.logical_not(scatters))
        def _():
            signal(barrier, p, partner)

        pl.semaphore_wait(barrier, greetings(STEPS0, edge0, (1, -1)) * count(flows) + 1 + (NC - 1) * count(scatters))

        @pl.when(flows)
        def _():
            answer(STEPS0, edge0, ready0)

    @pl.when(is_one)
    def _():
        greet(STEPS1, edge1)

        for s in (1, -1):
            parent = wrap(p - s)

            @pl.when(flows & edge0(s, parent) & (parent > p))
            def _():
                signal(barrier, parent, partner)

        for step in (1, -1):
            signal(barrier, p, 2 * (chip_y * SIDE + lax.rem(chip_x + step + SIDE, SIDE)) + 1)
            signal(barrier, p, 2 * (lax.rem(chip_y + step + SIDE, SIDE) * SIDE + chip_x) + 1)

        for t in range(PANELS):

            @pl.when((partner != t) & (q != t))
            def _():
                signal(barrier, p, t)

        @pl.when(q == 1)
        def _():
            @pl.loop(1, NC)
            def _(j):
                signal(barrier, p, 2 * j + 1)

        signal(barrier, p, partner)
        others = 4 + 4 - count((partner == 0) | (partner == 2)) + (NC - 2) * count(q == 1)
        pl.semaphore_wait(barrier, greetings(STEPS1, edge1) + others)
        answer(STEPS1, edge1, ready1)

    fetch.wait()

    def scatter(t, b):
        k = lax.rem(q, PANELS)
        return remote(x_ref.at[b, :, t], rs.at[k, b], sc_send.at[b], sc_recv.at[b, k], p, 2 * t + 1)

    def own(half):
        piece = cols.at[1, lax.rem(p, PANELS), half]
        return remote(x_ref.at[0, half], piece, own_send.at[half], own_recv.at[half], p, partner)

    @pl.when(is_one & is_root & flows)
    def _():
        own(0).start()
        own(1).start()

    @pl.when(q < PANELS)
    def _():
        for b in range(2):

            @pl.loop(0, NC)
            def _(t):
                @pl.when(2 * t + 1 != q)
                def _():
                    scatter(t, b).start()

    def col_piece(k, i):
        half, j = i // 4, lax.rem(i, 4)
        return cols.at[j // 2, k, half, pl.ds(lax.rem(j, 2) * (CR // S), CR // S)]

    def col_copy(k, half, i, step, slot=None):
        piece = col_piece(k, i)
        n = STEPS0.index(step)
        to = q + lax.rem(i, 4) // 2 if step in (1, -1) else q
        send = sends.at[(k * 2 + half) * 4 + n if slot is None else slot]
        return remote(piece, piece, send, z_recv.at[k * CHUNKS + i], wrap(p + step), to)

    def to_one(k, i):
        piece = col_piece(k, i)
        return remote(piece, piece, zc_send.at[k], zc_recv.at[k], p, partner)

    def live(i):
        return (chip > 1) | (lax.rem(i, 4) >= 2)

    def pass_on(k, i):
        away = wrap(p - k)
        for half in range(2):

            @pl.when(i // 4 == half)
            def _():
                for s in STEPS0:

                    @pl.when(among(away, ON[half][s]))
                    def _():
                        col_copy(k, half, i, s).start()

    def passed(k):
        away = wrap(p - k)
        for half in range(2):
            for n, s in enumerate(STEPS0):
                places = among(away, ON[half][s])
                for flag, piece in ((chip > 1, cols.at[:, k, half]), (chip == 1, cols.at[1, k, half])):

                    @pl.when(places & flag)
                    def _():
                        remote(piece, piece, sends.at[(k * 2 + half) * 4 + n], z_recv.at[0], p, partner).wait_send()

    def in_turn(k, i):
        away = wrap(p - k)
        return lax.rem(i + 4 * count(away > 8), CHUNKS)

    @pl.when(is_zero & flows)
    def _():
        mine = lax.rem(p, PANELS)

        def own_copy(n, step):
            i = lax.rem(n + (0 if step == 2 else 4), CHUNKS)
            return col_copy(mine, 0, i, step, 6 * 4 + (0 if step == 2 else WINDOW) + lax.rem(n, WINDOW))

        def start_own(n, step):
            @pl.when(is_root & (n < CHUNKS) & live(n))
            def _():
                @pl.when((n >= WINDOW) & live(n + CHUNKS - WINDOW))
                def _():
                    own_copy(n - WINDOW, step).wait_send()

                own_copy(n, step).start()

        @pl.when(is_root)
        def _():
            cols[0, mine] = x_ref[0]

        await_ready(STEPS0, edge0, ready0, 2)

        @pl.loop(0, CHUNKS + LAG)
        def _(n):
            for half, turn in ((0, 2), (1, LAG + 2)):

                @pl.when(is_root & (n == turn))
                def _():
                    own(half).wait_recv()

            start_own(n, 2)

            @pl.when(n == LAG)
            def _():
                for s in (-2, -1, 1):
                    await_ready(STEPS0, edge0, ready0, s)

            @pl.when(n >= LAG)
            def _():
                i = n - LAG
                start_own(i, -2)
                for k in reversed(range(PANELS)):
                    away = wrap(p - k)

                    @pl.when((lax.rem(away, 2) == 0) & (away != 0) & live(i))
                    def _():
                        t = in_turn(k, i)
                        col_copy(k, 0, t, 2).wait_recv()
                        pass_on(k, t)

                        @pl.when(lax.rem(t, 4) >= 2)
                        def _():
                            to_one(k, t).start()

        @pl.when(is_root)
        def _():
            @pl.loop(0, CHUNKS)
            def _(n):
                @pl.when(live(n) & ((n >= CHUNKS - WINDOW) | jnp.logical_not(live(n + WINDOW))))
                def _():
                    own_copy(n, 2).wait_send()
                    own_copy(n, -2).wait_send()

    def await_fills():
        @pl.when(flows)
        def _():
            for k in range(PANELS):

                @pl.when((lax.rem(wrap(p - k), 2) == 1) & (is_one | (chip > 1)))
                def _():
                    @pl.loop(0, CHUNKS // 2)
                    def _(i):
                        col_copy(k, 0, (i // 2) * 4 + core * 2 + lax.rem(i, 2), 2).wait_recv()

                @pl.when(is_one & (p != k) & (lax.rem(wrap(p - k), 2) == 0))
                def _():
                    remote(cols.at[1, k], cols.at[1, k], zc_send.at[k], zc_recv.at[k], p, partner).wait_recv()

    @pl.when((chip == 0) | ((chip == 1) & is_zero))
    def _():
        cols[core] = jnp.zeros_like(cols[core])

    def across(buffer, n, half, c):
        piece = buffer.at[half, c]
        return remote(piece, piece, cc_send.at[n], cc_recv.at[n], p, partner)

    def whole(buffer, n):
        return remote(buffer, buffer, cc_send.at[n], cc_recv.at[n], p, partner)

    class Ring:
        def __init__(self, buffer, recv, n, apart):
            self.buffer, self.recv, self.n, self.apart = buffer, recv, n, apart

        def line(self, stage, half, t, step):
            if stage == half:
                x = lax.rem(chip_x + step + SIDE, SIDE)
                return (chip_y if stage == 0 else t) * SIDE + x
            y = lax.rem(chip_y + step + SIDE, SIDE)
            return y * SIDE + (chip_x if stage == 0 else t)

        def neighbour(self, stage, half, step):
            if stage == half:
                return 2 * (chip_y * SIDE + lax.rem(chip_x + step + SIDE, SIDE)) + 1
            return 2 * (lax.rem(chip_y + step + SIDE, SIDE) * SIDE + chip_x) + 1

        def copy(self, stage, half, t, kind):
            step = 1 if kind in (0, 2) else -1
            piece = self.buffer.at[half, self.line(stage, half, t, 0 if kind < 2 else -step)]
            if kind >= 2:
                piece = piece.at[:, :, :, pl.ds((kind - 2) * (B // 2), B // 2)]
            return self.between(piece, stage, half, t, kind, self.neighbour(stage, half, step))

        def between(self, piece, stage, half, t, kind, to):
            i = kind * 4 + stage * 2 + half
            recv = self.recv.at[i]
            if self.apart and stage == 1 and kind < 2:
                recv = self.recv.at[16 + (kind * 2 + half) * SIDE + t]
            return remote(piece, piece, sends.at[self.n * 16 + i], recv, p, to)

        def all_of(self, stage, half, kind):
            piece = self.buffer.at[half, pl.ds(0, SIDE if stage else 1)]
            if kind >= 2:
                piece = piece.at[:, :, :, :, pl.ds(0, B // 2)]
            return self.between(piece, stage, half, 0, kind, partner)

        def each(self, stage, act, offsets=(0, 1, 3, 2)):
            for offset in offsets if stage else (0,):
                for half in range(2):
                    act(half, lax.rem((chip_y if half else chip_x) + offset, SIDE) if stage else 0)

        def push(self, stage, half, t, step):
            if stage == 1:
                across(self.buffer, self.n, half, self.line(stage, half, t, step)).start()

        def begin(self, stage, offsets=(0, 1, 3, 2)):
            def act(half, t):
                self.copy(stage, half, t, 0).start()
                self.copy(stage, half, t, 1).start()
                self.push(stage, half, t, 0)

            self.each(stage, act, offsets)

        def middle(self, stage):
            apart = self.apart and stage == 1
            if not apart:
                for half in range(2):
                    for kind in range(2):
                        self.all_of(stage, half, kind).wait_recv()

            def act(half, t):
                for kind in range(2):
                    if apart:
                        self.copy(stage, half, t, kind).wait_recv()
                    self.copy(stage, half, t, 2 + kind).start()
                    self.push(stage, half, t, -1 if kind == 0 else 1)

            self.each(stage, act)

        def end(self, stage):
            for half in range(2):
                for kind in (2, 3):
                    self.all_of(stage, half, kind).wait_recv()
            self.each(stage, lambda half, t: self.push(stage, half, t, 2))

        def sent(self):
            for stage in range(2):
                for half in range(2):
                    for kind in range(4):
                        self.all_of(stage, half, kind).wait_send()

    near = lax.rem(p, 4)
    mine4 = lax.rem(near, PANELS)
    anchor = near < PANELS

    def along(step):
        n = STEPS1.index(step)
        return remote(hs.at[mine4], hs.at[mine4], hz_send.at[n], hz_recv.at[mine4], wrap(p + step), q)

    row_ring = Ring(rows, ra_recv, 0, False)
    head_ring = Ring(head, ha_recv, 1, True)

    @pl.when(is_one)
    def _():
        @pl.when(q == 1)
        def _():
            rs[1] = x_ref[:, :, 0]

        def scattered(b):
            for k in range(PANELS):

                @pl.when(q != k)
                def _():
                    remote(x_ref.at[b, :, 0], rs.at[k, b], sc_send.at[b], sc_recv.at[b, k], p, partner).wait_recv()

        @pl.when(is_root)
        def _():
            scattered(0)
            hs[mine4] = rs[:, 0]

        @pl.when(anchor & jnp.logical_not(is_root))
        def _():
            along(4).wait_recv()

        for s in STEPS1:
            await_ready(STEPS1, edge1, ready1, s)

            @pl.when(edge1(s, p))
            def _():
                along(s).start()

        @pl.when(jnp.logical_not(is_root))
        def _():
            scattered(0)

        scattered(1)
        for half in range(2):
            rows[half, chip] = rs[:, :, half]
        row_ring.begin(0)

        for k in range(PANELS):

            @pl.when(near != k)
            def _():
                remote(hs.at[k], hs.at[k], hz_send.at[0], hz_recv.at[k], p, partner).wait_recv()

        for half in range(2):
            head[half, chip] = hs[:, :, half]
        head_ring.begin(0)
        head_ring.begin(1, (0,))
        head_ring.middle(0)
        head_ring.begin(1, (1, 3))
        head_ring.end(0)
        head_ring.begin(1, (2,))
        row_ring.middle(0)

        @pl.when(is_root & flows)
        def _():
            cols[1, lax.rem(p, PANELS)] = x_ref[0]

        head_ring.middle(1)
        row_ring.end(0)
        row_ring.begin(1)
        head_ring.end(1)

    @pl.when(is_zero)
    def _():
        whole(head, 1).wait_recv()

    def block(i, j):
        return head[:, :, i, j].reshape(B, B)

    a = {(i, j): block(i, j) for i in range(PANELS) for j in range(PANELS)}
    halves = {}
    for k in range(PANELS):
        inverse = invert(a[k, k])
        fact[k, k] = inverse
        halves[k, k] = split(inverse)
        below = range(k + 1, PANELS)
        if below:
            for i, factor in zip(below, products([split(a[i, k]) for i in below], halves[k, k])):
                fact[i, k] = factor
                halves[i, k] = split(factor)
        for j in below:
            fact[k, j] = a[k, j]
            halves[k, j] = split(a[k, j])
            for i, update in zip(below, products([halves[i, k] for i in below], halves[k, j])):
                a[i, j] = a[i, j] - update
        if k == 1:

            @pl.when(is_one)
            def _():
                row_ring.middle(1)

    await_fills()
    is_panel = q < PANELS
    eye = (
        lax.broadcasted_iota(jnp.int32, (B, B), 0) == lax.broadcasted_iota(jnp.int32, (B, B), 1)
    ).astype(jnp.float32)
    value = [cols[core, i].reshape(B, B) for i in range(PANELS)]
    for i in range(PANELS):
        upper[i] = value[i]
        later = range(i + 1, PANELS)
        if later:
            for m, update in zip(later, products([halves[m, i] for m in later], split(value[i]))):
                value[m] = value[m] - update

    right = [None] * PANELS
    value = [jnp.where(is_panel, jnp.where(q == i, eye, 0.0), upper[i]) for i in range(PANELS)]
    for i in reversed(range(PANELS)):
        right[i] = split(product(halves[i, i], split(value[i])))
        if i:
            for m, update in zip(range(i), products([halves[m, i] for m in range(i)], right[i])):
                value[m] = value[m] - update

    @pl.when(is_one)
    def _():
        row_ring.end(1)

    @pl.when(is_zero)
    def _():
        whole(rows, 0).wait_recv()

    keep = jnp.where(is_panel, 0.0, 1.0)
    sign = jnp.where(is_panel, 1.0, -1.0)
    total = [None, None]
    for k in range(PANELS):
        panel = [split(rows[:, :, k, b].reshape(B, B)) for b in range(2)]
        for b, term in enumerate(products(panel, right[k])):
            total[b] = term if k == 0 else total[b] + term
    def store(b):
        return pltpu.make_async_copy(out_ref.at[b], out_hbm.at[b], io.at[1 + b])

    out_ref[1] = keep * x_ref[1].reshape(B, B) + sign * total[1]
    store(1).start()

    @pl.when(jnp.logical_not(is_root))
    def _():
        out_ref[0] = keep * x_ref[0].reshape(B, B) + sign * total[0]

    @pl.when(is_root & is_panel)
    def _():
        out_ref[0] = fact[lax.rem(p, PANELS), lax.rem(q, PANELS)]

    @pl.when(is_root & (q >= PANELS))
    def _():
        out_ref[0] = upper[lax.rem(p, PANELS)]

    store(0).start()

    for b in range(2):
        for pieces, flag in ((NC - 1, q == 1), (NC, scatters)):

            @pl.when(flag)
            def _():
                piece = x_ref.at[b, :, pl.ds(0, pieces)]
                remote(piece, piece, sc_send.at[b], sc_recv.at[b, 0], p, partner).wait_send()

    @pl.when(is_zero & flows)
    def _():
        for k in range(PANELS):

            @pl.when(p != k)
            def _():
                passed(k)

            @pl.when((p != k) & (lax.rem(wrap(p - k), 2) == 0))
            def _():
                remote(cols.at[1, k], cols.at[1, k], zc_send.at[k], zc_recv.at[k], p, partner).wait_send()

    @pl.when(is_one)
    def _():
        @pl.when(is_root & flows)
        def _():
            own(0).wait_send()
            own(1).wait_send()

        for s in STEPS1:

            @pl.when(edge1(s, p))
            def _():
                along(s).wait_send()

        row_ring.sent()
        head_ring.sent()
        whole(rows, 0).wait_send()
        whole(head, 1).wait_send()

    store(0).wait()
    store(1).wait()


def body(matrix):
    shape = matrix.shape
    f32 = jnp.float32
    dma = pltpu.SemaphoreType.DMA
    out = pl.pallas_call(
        kernel,
        out_shape=jax.ShapeDtypeStruct((2, B, B), f32),
        in_specs=[pl.BlockSpec(memory_space=pl.ANY)],
        out_specs=pl.BlockSpec(memory_space=pl.ANY),
        scratch_shapes=[
            pltpu.VMEM((2, 2, NC, S, B), f32),
            pltpu.VMEM((2, B, B), f32),
            pltpu.VMEM((PANELS, 2, 2, S, B), f32),
            pltpu.VMEM((2, NC, PANELS, 2, S, B), f32),
            pltpu.VMEM((PANELS, PANELS, 2, S, B), f32),
            pltpu.VMEM((2, NC, PANELS, PANELS, S, B), f32),
            pltpu.VMEM((2, PANELS, 2, NC, S, B), f32),
            pltpu.VMEM((PANELS, PANELS, B, B), f32),
            pltpu.VMEM((PANELS, B, B), f32),
            pltpu.SemaphoreType.REGULAR((len(STEPS0),)),
            pltpu.SemaphoreType.REGULAR((len(STEPS1),)),
            dma((3,)),
            dma((2,)),
            dma((2, PANELS)),
            dma((32,)),
            dma((16,)),
            dma((32,)),
            dma((len(STEPS1),)),
            dma((PANELS,)),
            dma((PANELS * CHUNKS,)),
            dma((2,)),
            dma((2,)),
            dma((PANELS,)),
            dma((PANELS,)),
            dma((2,)),
            dma((2,)),
        ],
        compiler_params=pltpu.CompilerParams(
            collective_id=0, has_side_effects=True, vmem_limit_bytes=48 * 1024 * 1024
        ),
    )(matrix.reshape(2, 2, NC, S, B))
    return out.reshape(shape)


def solution(mesh):
    spec = P(None, "prow", None, "pcol", None)
    return jax.shard_map(body, mesh=mesh, in_specs=(spec,), out_specs=spec, check_vma=False)
```
